256 devices in a mesh: section: 16 (over y, z_lo), tensor: 8 (over x, core), group: 2 (over z_hi).
Axes of the slice: x: 4, y: 4, z: 8 (z_hi: 2, z_lo: 4; z = z_hi * 4 + z_lo), core: 2. Of those that a mesh axis runs over, the one named last changes fastest.
Arguments:
- ref_input: bfloat16 [2, 2, 128, 16384], P('group', None, None, 'tensor'), may hold values from -40 to 40
- norm_gain: float32 [16, 16384], P('section', 'tensor'), may hold values from 0.1 to 1.9
- w_in: bfloat16 [16, 16384, 768], P('section', 'tensor'), may hold values from -0.046875 to 0.046875
- w_out: bfloat16 [16, 384, 16384], P('section', None, 'tensor'), may hold values from -0.3125 to 0.3125
- policy_hidden: bfloat16 [512, 16384], P('group', 'tensor'), may hold values from -40 to 40
- heads: bfloat16 [2, 16384, 16384], P('group', 'section', 'tensor'), may hold values from -1 to 1
- sampled: int32 [512], replicated, may hold values from 0 to 16383
- live_mask: int32 [512], replicated, may hold values 0 or 1
- rewards: float32 [8], replicated, may hold values from -8 to 8
- prompt_ids: int32 [8], replicated, may hold values from 0 to 1, as said below
Outputs:
- token_kl: float32 [512], P(('tensor', 'group'))
- token_loss: float32 [512], P(('tensor', 'group'))
The draws below stay inside these ranges and needn't reach their ends.
Inputs may be any that keep to these rules, and one draw needn't show every extreme that they name: `prompt_ids`: each of the 2 prompts is answered by exactly 4 responses.
All inputs are finite; a program needn't handle non-finite values.
Results may differ from the reference program's by a relative error of at most 0.017.
Values may be sent and summed in bfloat16 or wider, within the bound.
A program may use at most 64 MiB of HBM per device.

```python
import math
import jax
import jax.numpy as jnp
from jax import lax

D = 16384
V = 16384
FW = 384
R = 128
MB = 2
RLEN = 64
GSIZE = 4
LAYERS = 16
TOKENS = 512
NRESP = 8


def spread_levels(key, shape, lower, upper):
    return lower * (upper / lower) ** jax.random.uniform(key, shape, jnp.float32)


def activation_block(key, shape, base):
    key_row, key_col = jax.random.split(key, 2)
    leading = shape[:-1] + (1,)
    row_scale = spread_levels(key_row, leading, 0.3, 3.0)
    rising = 3.0 ** (jnp.arange(D, dtype=jnp.float32) / D)
    col_scale = spread_levels(key_col, (D,), 0.3, 1.0) * rising
    values = base * row_scale * col_scale
    return jnp.clip(values, -40.0, 40.0)


def draw_ref_input(key, part):
    key = jax.random.fold_in(key, 1)
    key_base, key_rest = jax.random.split(key)
    shape = (2, MB, R, D)
    base = jax.random.normal(key_base, shape, jnp.float32)
    return activation_block(key_rest, shape, base).astype(jnp.bfloat16)


def draw_policy_hidden(key, part):
    key = jax.random.fold_in(key, 2)
    key_base, key_rest = jax.random.split(key)
    shape = (TOKENS, D)
    base = jax.random.normal(key_base, shape, jnp.float32)
    return activation_block(key_rest, shape, base).astype(jnp.bfloat16)


def draw_heads(key, part):
    key = jax.random.fold_in(key, 3)
    key_base, key_row = jax.random.split(key, 2)
    shape = (2, V, D)
    base = jax.random.normal(key_base, shape, jnp.float32)
    rising = 3.0 ** (jnp.arange(V, dtype=jnp.float32) / V)
    row_scale = spread_levels(key_row, (2, V, 1), 0.3, 3.0) * rising[None, :, None]
    values = base * row_scale * (3.0 / math.sqrt(D))
    return jnp.clip(values, -1.0, 1.0).astype(jnp.bfloat16)


def draw_prompt_ids(key, part):
    key = jax.random.fold_in(key, 4)
    owners = jnp.arange(NRESP, dtype=jnp.int32) // GSIZE
    return jax.random.permutation(key, owners).astype(jnp.int32)


def plant(array, own_key, least, high):
    longest = array.shape.index(max(array.shape))
    spots = []
    for shift in (0, 1):
        where = [jax.random.randint(jax.random.fold_in(own_key, axis), (), 0, length) for axis, length in enumerate(array.shape)]
        where[longest] = (where[longest] + shift) % array.shape[longest]
        spots.append(tuple(where))
    return array.at[spots[0]].set(least).at[spots[1]].set(high)


def block_levels(key, dims, cuts, low, top_value):
    def one(axis_at, blocks):
        draws = jax.random.uniform(jax.random.fold_in(jax.random.fold_in(key, 6), axis_at), (blocks,), jnp.float32, low / len(cuts), top_value / len(cuts))
        return jnp.repeat(jnp.exp(draws), dims[axis_at] // blocks).reshape((-1,) + (1,) * (len(dims) - axis_at - 1))

    loudness = one(*cuts[0])
    for cut in cuts[1:]:
        loudness = loudness * one(*cut)
    return loudness


def normal_values(rng, extent, width, most, pieces=(), held_as=jnp.bfloat16):
    array = width * jax.random.normal(rng, extent, jnp.float32)
    if pieces:
        array = array * block_levels(rng, extent, pieces, -0.22, 0.18)
    return jnp.clip(array, -most, most).astype(held_as)


def setup_inputs(seed: int = 0) -> dict:
    seeds = jax.random.split(jax.random.key(seed), 11)
    ref_input = draw_ref_input(jax.random.fold_in(seeds[10], 71), 0)
    norm_gain = jnp.clip(1.0 + 0.18 * jax.random.normal(seeds[1], (LAYERS, D), jnp.float32), 0.1, 1.9)
    w_in = normal_values(seeds[2], (LAYERS, D, 2 * FW), D ** -0.5, 0.046875, ((0, 16), (1, 8)))
    w_out = normal_values(seeds[3], (LAYERS, FW, D), FW ** -0.5, 0.3125, ((0, 16), (2, 8)))
    policy_hidden = draw_policy_hidden(jax.random.fold_in(seeds[10], 71), 0)
    heads = draw_heads(jax.random.fold_in(seeds[10], 71), 0)
    sampled = plant(jax.random.randint(seeds[6], (TOKENS,), 0, V), jax.random.fold_in(seeds[6], 1), 0, V - 1).astype(jnp.int32)
    live_mask = plant((jax.random.randint(seeds[7], (TOKENS,), 0, 4) < 3).astype(jnp.int32), jax.random.fold_in(seeds[7], 1), 0, 1)
    rewards = normal_values(seeds[8], (NRESP,), 2.0, 8.0, (), jnp.float32)
    prompt_ids = draw_prompt_ids(jax.random.fold_in(seeds[10], 71), 0)
    return {"ref_input": ref_input, "norm_gain": norm_gain, "w_in": w_in, "w_out": w_out, "policy_hidden": policy_hidden, "heads": heads, "sampled": sampled, "live_mask": live_mask, "rewards": rewards, "prompt_ids": prompt_ids}


epsilon = 1e-05
penalty = 0.04

def apply_layer(stream, gain_row, weight_in, weight_out):
    values = stream.astype(jnp.float32)
    squares = lax.optimization_barrier(jnp.mean(values * values, axis=1, keepdims=True))
    normed = (values * lax.rsqrt(squares + epsilon) * gain_row[None, :]).astype(jnp.bfloat16)
    mixed = jnp.dot(normed, weight_in, preferred_element_type=jnp.float32)
    units = weight_out.shape[0]
    hidden = (jax.nn.silu(mixed[:, :units]) * mixed[:, units:]).astype(jnp.bfloat16)
    update = jnp.dot(hidden, weight_out, preferred_element_type=jnp.float32)
    return (values + update).astype(jnp.bfloat16)

def advantages(rewards, prompt_ids):
    same = (prompt_ids[:, None] == prompt_ids[None, :]).astype(jnp.float32)
    counts = lax.optimization_barrier(jnp.sum(same, axis=1))
    means = lax.optimization_barrier(jnp.sum(same * rewards[None, :], axis=1)) / counts
    spread = rewards[None, :] - means[:, None]
    variance = lax.optimization_barrier(jnp.sum(same * spread * spread, axis=1)) / counts
    return (rewards - means) / jnp.maximum(jnp.sqrt(variance), 1.0)

def reference(ref_input, norm_gain, w_in, w_out, policy_hidden, heads, sampled, live_mask, rewards, prompt_ids):
    stream = ref_input.reshape(TOKENS, D)
    for layer_index in range(LAYERS):
        stream = apply_layer(stream, norm_gain[layer_index], w_in[layer_index], w_out[layer_index])
    ref_logits = jnp.dot(stream, heads[0].T, preferred_element_type=jnp.float32)
    pol_logits = jnp.dot(policy_hidden, heads[1].T, preferred_element_type=jnp.float32)
    peak_pol = lax.optimization_barrier(jnp.max(pol_logits, axis=1))
    peak_ref = lax.optimization_barrier(jnp.max(ref_logits, axis=1))
    weights_pol = jnp.exp(pol_logits - peak_pol[:, None])
    weights_ref = jnp.exp(ref_logits - peak_ref[:, None])
    total_pol = lax.optimization_barrier(jnp.sum(weights_pol, axis=1))
    total_ref = lax.optimization_barrier(jnp.sum(weights_ref, axis=1))
    cross = lax.optimization_barrier(jnp.sum(weights_pol * (pol_logits - ref_logits), axis=1))
    lse_pol = peak_pol + jnp.log(total_pol)
    lse_ref = peak_ref + jnp.log(total_ref)
    token_kl = cross / total_pol - lse_pol + lse_ref
    chosen = jnp.take_along_axis(pol_logits, sampled[:, None].astype(jnp.int32), axis=1)[:, 0]
    log_prob = chosen - lse_pol
    token_adv = jnp.repeat(advantages(rewards, prompt_ids), RLEN)
    live = live_mask.astype(jnp.float32)
    token_loss = live * (penalty * token_kl - token_adv * log_prob) / RLEN
    return (token_kl, token_loss)
```

```python
import functools

import jax
import jax.numpy as jnp
from jax import lax
from jax.experimental import pallas as pl
from jax.experimental.pallas import tpu as pltpu
from jax.sharding import PartitionSpec as P

RLEN = 64
ROWS = 16
HALF = 8
SIDE = 4

epsilon = 1e-05
penalty = 0.04
MESH = pl.DeviceIdType.MESH


def as_count(flag):
    return jnp.where(flag, 1, 0).astype(jnp.int32)


def tree_edges(section, group):
    last = SIDE - 1
    row, column = section // SIDE, section % SIDE

    def at(r, c):
        return jnp.logical_and(row == r, column == c)

    def tree(mirror):
        place = (lambda c: last - c) if mirror else (lambda c: c)
        step = 1 if mirror else -1

        def here(r, c):
            return at(r, place(c))

        def any_of(spots):
            flag = here(*spots[0])
            for spot in spots[1:]:
                flag = jnp.logical_or(flag, here(*spot))
            return flag

        low_rows = row < last
        along = (
            jnp.logical_or(
                jnp.logical_and(low_rows, column != place(0)),
                here(last, last),
            ),
            section + step,
            jnp.logical_or(
                jnp.logical_and(low_rows, column != place(last)),
                here(last, last - 1),
            ),
            section - step,
        )
        up = (
            any_of([(3, 3), (0, 3), (2, 1), (2, 0)]),
            ((row + 1) % SIDE) * SIDE + column,
            any_of([(0, 3), (1, 3), (3, 1), (3, 0)]),
            ((row + SIDE - 1) % SIDE) * SIDE + column,
        )
        down = (
            here(3, 3),
            ((row + SIDE - 1) % SIDE) * SIDE + column,
            here(2, 3),
            ((row + 1) % SIDE) * SIDE + column,
        )
        return [along, up, down]

    return tree(False), tree(True)


def relay_kernel(
    x_ref, gain_ref, win_ref, wout_ref, out_ref,
    stream, partial, pieces, mine, twin_rows, leaving,
    piece_send, piece_recv, twin_send, twin_recv, stream_send, stream_recv, final_send, final_recv,
):
    batches = x_ref.shape[0]
    width = x_ref.shape[2]
    units = wout_ref.shape[0]
    tensor_count = lax.axis_size("tensor")
    section_count = lax.axis_size("section")
    section = lax.axis_index("section")
    tensor = lax.axis_index("tensor")
    group = lax.axis_index("group")
    core = tensor % 2
    twin = tensor + 1 - 2 * core
    first_section = section == 0
    last_section = section == section_count - 1
    in_first = group == 0
    tree_a, tree_b = tree_edges(section, group)
    entry = SIDE * (SIDE - 1)
    crossing_out = jnp.logical_and(last_section, group == 1)
    crossing_in = jnp.logical_and(section == entry, in_first)

    barrier = pltpu.get_barrier_semaphore()
    expected = jnp.int32(tensor_count - 1)
    for offset in range(1, tensor_count):
        pl.semaphore_signal(
            barrier, 1, device_id={"tensor": (tensor + offset) % tensor_count}, device_id_type=MESH
        )

    def greet(flag, where):
        @pl.when(flag)
        def _():
            pl.semaphore_signal(barrier, 1, device_id=where, device_id_type=MESH)

        return as_count(flag)

    expected += greet(jnp.logical_not(last_section), {"section": section + 1})
    expected += greet(jnp.logical_not(first_section), {"section": section - 1})
    for sends, target, receives, source in tree_a + tree_b:
        expected += greet(jnp.logical_and(in_first, sends), {"section": target})
        expected += greet(jnp.logical_and(in_first, receives), {"section": source})
    expected += greet(crossing_out, {"section": entry, "group": 0})
    expected += greet(crossing_in, {"section": section_count - 1, "group": 1})
    pl.semaphore_wait(barrier, expected)

    def piece_copy(batch, offset):
        target = (tensor + offset) % tensor_count
        return pltpu.make_async_remote_copy(
            src_ref=partial.at[batch, target % 2],
            dst_ref=pieces.at[batch, offset - 1],
            send_sem=piece_send.at[batch],
            recv_sem=piece_recv.at[batch],
            device_id={"tensor": target},
            device_id_type=MESH,
        )

    def twin_copy(batch):
        return pltpu.make_async_remote_copy(
            src_ref=mine.at[batch],
            dst_ref=twin_rows.at[batch],
            send_sem=twin_send.at[batch],
            recv_sem=twin_recv.at[batch],
            device_id={"tensor": twin},
            device_id_type=MESH,
        )

    def stream_copy(batch):
        return pltpu.make_async_remote_copy(
            src_ref=leaving.at[batch],
            dst_ref=stream.at[batch],
            send_sem=stream_send.at[batch],
            recv_sem=stream_recv.at[batch],
            device_id={"section": section + 1},
            device_id_type=MESH,
        )

    def final_copy(source, slot, edge, where):
        return pltpu.make_async_remote_copy(
            src_ref=source,
            dst_ref=out_ref.at[slot],
            send_sem=final_send.at[slot, edge],
            recv_sem=final_recv.at[slot],
            device_id=where,
            device_id_type=MESH,
        )

    def stage_a(batch):
        @pl.when(first_section)
        def _():
            stream[batch] = x_ref[batch]

        @pl.when(jnp.logical_not(first_section))
        def _():
            stream_copy(batch).wait_recv()

        values = stream[batch].astype(jnp.float32)
        squares = jnp.sum(values * values, axis=1, keepdims=True)
        scaled = (values * gain_ref[...]).astype(jnp.bfloat16)
        mixed = jnp.dot(scaled, win_ref[...], preferred_element_type=jnp.float32)
        squares = jnp.broadcast_to(squares, (ROWS, 128))
        coarse = squares.astype(jnp.bfloat16).astype(jnp.float32)
        fine = squares - coarse
        for half in range(2):
            rows = slice(half * HALF, (half + 1) * HALF)
            partial[batch, half, :, :units] = jnp.concatenate(
                [mixed[rows, :units], mixed[rows, units:]], 0
            ).astype(jnp.bfloat16)
            partial[batch, half, :, units:] = jnp.concatenate(
                [coarse[rows], fine[rows]], 0
            ).astype(jnp.bfloat16)
        for offset in range(1, tensor_count):
            piece_copy(batch, offset).start()

    def stage_b(batch):
        pltpu.make_async_copy(pieces.at[batch], pieces.at[batch], piece_recv.at[batch]).wait()
        total = partial[batch, core].astype(jnp.float32)
        for offset in range(1, tensor_count):
            total += pieces[batch, offset - 1].astype(jnp.float32)
        squares = total[:HALF, units:units + 1] + total[HALF:, units:units + 1]
        scale = lax.rsqrt(squares / (width * tensor_count) + epsilon)
        gate = total[:HALF, :units] * scale
        up = total[HALF:, :units] * scale
        mine[batch] = gate / (1.0 + jnp.exp(-gate)) * up
        twin_copy(batch).start()

    def stage_c(batch):
        twin_copy(batch).wait_recv()
        here, there = mine[batch], twin_rows[batch]
        hidden = jnp.concatenate(
            [jnp.where(core == 0, here, there), jnp.where(core == 0, there, here)], 0
        ).astype(jnp.bfloat16)
        update = jnp.dot(hidden, wout_ref[...], preferred_element_type=jnp.float32)
        leaving[batch] = (stream[batch].astype(jnp.float32) + update).astype(jnp.bfloat16)

        @pl.when(jnp.logical_not(last_section))
        def _():
            stream_copy(batch).start()

        @pl.when(jnp.logical_and(last_section, in_first))
        def _():
            out_ref[batch] = leaving[batch]
            for edge, (_, target, _, _) in enumerate(tree_a):
                final_copy(leaving.at[batch], batch, edge, {"section": target}).start()

        @pl.when(crossing_out)
        def _():
            final_copy(
                leaving.at[batch], batches + batch, 0, {"section": entry, "group": 0}
            ).start()

    def step(index, carry):
        @pl.when(index < batches)
        def _():
            stage_a(index)

        @pl.when(index >= 2)
        def _():
            stage_c(index - 2)

        @pl.when(jnp.logical_and(index >= 1, index <= batches))
        def _():
            stage_b(index - 1)

        return carry

    lax.fori_loop(0, batches + 2, step, 0)

    def forward(batch, carry):
        for first, edges in ((0, tree_a), (batches, tree_b)):
            slot = first + batch
            root = jnp.logical_and(last_section, first == 0)

            @pl.when(jnp.logical_and(in_first, jnp.logical_not(root)))
            def _(slot=slot, edges=edges):
                pltpu.make_async_copy(
                    out_ref.at[slot], out_ref.at[slot], final_recv.at[slot]
                ).wait()
                for edge, (sends, target, _, _) in enumerate(edges):
                    @pl.when(sends)
                    def _(edge=edge, target=target):
                        final_copy(out_ref.at[slot], slot, edge, {"section": target}).start()

        return carry

    lax.fori_loop(0, batches, forward, 0)

    def drain(batch, carry):
        pltpu.make_async_copy(pieces.at[batch], pieces.at[batch], piece_send.at[batch]).wait()
        twin_copy(batch).wait_send()

        @pl.when(jnp.logical_not(last_section))
        def _():
            stream_copy(batch).wait_send()

        for first, edges in ((0, tree_a), (batches, tree_b)):
            slot = first + batch
            for edge, (sends, target, _, _) in enumerate(edges):
                @pl.when(jnp.logical_and(in_first, sends))
                def _(edge=edge, target=target, slot=slot):
                    final_copy(out_ref.at[slot], slot, edge, {"section": target}).wait_send()

        @pl.when(crossing_out)
        def _():
            final_copy(
                leaving.at[batch], batches + batch, 0, {"section": entry, "group": 0}
            ).wait_send()

        return carry

    lax.fori_loop(0, batches, drain, 0)


def relay(rows, gain, weight_in, weight_out):
    tensor_count = lax.axis_size("tensor")
    batches, _, width = rows.shape
    units = weight_out.shape[0]
    piece = (ROWS, units + 128)
    dma = pltpu.SemaphoreType.DMA
    vmem = pl.BlockSpec(memory_space=pltpu.VMEM)
    return pl.pallas_call(
        relay_kernel,
        out_shape=jax.ShapeDtypeStruct((2 * batches, ROWS, width), jnp.bfloat16),
        in_specs=[vmem] * 4,
        out_specs=vmem,
        scratch_shapes=[
            pltpu.VMEM((batches, ROWS, width), jnp.bfloat16),
            pltpu.VMEM((batches, 2) + piece, jnp.bfloat16),
            pltpu.VMEM((batches, tensor_count - 1) + piece, jnp.bfloat16),
            pltpu.VMEM((batches, HALF, units), jnp.float32),
            pltpu.VMEM((batches, HALF, units), jnp.float32),
            pltpu.VMEM((batches, ROWS, width), jnp.bfloat16),
            dma((batches,)),
            dma((batches,)),
            dma((batches,)),
            dma((batches,)),
            dma((batches,)),
            dma((batches,)),
            dma((2 * batches, 3)),
            dma((2 * batches,)),
        ],
        compiler_params=pltpu.CompilerParams(
            collective_id=0, has_side_effects=True, vmem_limit_bytes=40 * 1024 * 1024
        ),
        name="relay",
    )(rows, gain, weight_in, weight_out)


def from_partner(block, axis):
    return lax.ppermute(block, axis, [(0, 1), (1, 0)])


def advantages(rewards, prompt_ids):
    same = (prompt_ids[:, None] == prompt_ids[None, :]).astype(jnp.float32)
    counts = jnp.sum(same, axis=1)
    means = jnp.sum(same * rewards[None, :], axis=1) / counts
    spread = rewards[None, :] - means[:, None]
    variance = jnp.sum(same * spread * spread, axis=1) / counts
    return (rewards - means) / jnp.maximum(jnp.sqrt(variance), 1.0)


def shards(
    ref_input, norm_gain, w_in, w_out, policy_hidden, heads, sampled, live_mask, rewards, prompt_ids
):
    section_here = lax.axis_index("section")
    group_here = lax.axis_index("group")
    first_group = group_here == 0
    width = ref_input.shape[3]
    rows = ref_input.reshape(-1, ROWS, width)
    policy_other = lax.ppermute(policy_hidden, "group", [(0, 1)])
    policy_rows = jnp.concatenate([policy_other, policy_hidden], 0)
    final = relay(rows, norm_gain, w_in[0], w_out[0]).reshape(-1, width)
    hidden_rows = jnp.where(first_group, final, policy_rows)
    logits = lax.psum_scatter(
        lax.dot_general(
            hidden_rows, heads[0], (((1,), (1,)), ((), ())), preferred_element_type=jnp.float32
        ),
        "tensor",
        scatter_dimension=0,
        tiled=True,
    )
    paired = lax.all_to_all(logits[None], "group", split_axis=1, concat_axis=0, tiled=True)
    reference_logits = paired[0]
    policy_logits = paired[1]
    local_rows = policy_logits.shape[0]
    vocab_block = policy_logits.shape[1]
    row_start = (lax.axis_index("tensor") * lax.axis_size("group") + group_here) * local_rows
    vocab_ids = section_here * vocab_block + lax.iota(jnp.int32, vocab_block)
    wanted = lax.dynamic_slice_in_dim(sampled, row_start, local_rows, 0)
    hits = vocab_ids[None, :] == wanted[:, None]
    picked = jnp.sum(jnp.where(hits, policy_logits, 0.0), axis=1)
    near_pol = jnp.max(policy_logits, axis=1)
    near_ref = jnp.max(reference_logits, axis=1)
    weights_pol = jnp.exp(policy_logits - near_pol[:, None])
    weights_ref = jnp.exp(reference_logits - near_ref[:, None])
    local_cross = jnp.sum(weights_pol * (policy_logits - reference_logits), axis=1)
    stats = jnp.stack(
        [near_pol, near_ref, jnp.sum(weights_pol, axis=1), jnp.sum(weights_ref, axis=1), local_cross, picked]
    )
    stats = lax.all_gather(stats, "section")
    peak_pol = jnp.max(stats[:, 0], axis=0)
    peak_ref = jnp.max(stats[:, 1], axis=0)
    shift_pol = jnp.exp(stats[:, 0] - peak_pol)
    shift_ref = jnp.exp(stats[:, 1] - peak_ref)
    total_pol = jnp.sum(shift_pol * stats[:, 2], axis=0)
    total_ref = jnp.sum(shift_ref * stats[:, 3], axis=0)
    cross = jnp.sum(shift_pol * stats[:, 4], axis=0)
    chosen = jnp.sum(stats[:, 5], axis=0)
    lse_pol = peak_pol + jnp.log(total_pol)
    lse_ref = peak_ref + jnp.log(total_ref)
    token_kl = cross / total_pol - lse_pol + lse_ref
    log_prob = chosen - lse_pol
    token_adv = lax.dynamic_slice_in_dim(
        jnp.repeat(advantages(rewards, prompt_ids), RLEN), row_start, local_rows, 0
    )
    live = lax.dynamic_slice_in_dim(live_mask, row_start, local_rows, 0).astype(jnp.float32)
    token_loss = live * (penalty * token_kl - token_adv * log_prob) / RLEN
    return (token_kl, token_loss)


def solution(mesh):
    in_specs = (
        P("group", None, None, "tensor"),
        P("section", "tensor"),
        P("section", "tensor", None),
        P("section", None, "tensor"),
        P("group", "tensor"),
        P("group", "section", "tensor"),
        P(),
        P(),
        P(),
        P(),
    )
    out_specs = (P(("tensor", "group")), P(("tensor", "group")))
    return jax.shard_map(shards, mesh=mesh, in_specs=in_specs, out_specs=out_specs, check_vma=False)
```

```python
import jax
import jax.numpy as jnp
from jax import lax
from jax.experimental import pallas as pl
from jax.experimental.pallas import tpu as pltpu
from jax.sharding import PartitionSpec as P

RLEN = 64
SIDE = 4
BLOCK = 16
ROWS = 32
HALF = ROWS // 2
PER = ROWS // BLOCK
CHUNK = 64
LANES = 128

epsilon = 1e-05
penalty = 0.04
MESH = pl.DeviceIdType.MESH


def as_count(flag):
    return jnp.where(flag, 1, 0).astype(jnp.int32)


def block_at(place):
    return (place % SIDE) * SIDE + place // SIDE


def tree_edges(section, mirror):
    last = SIDE - 1
    row, column = section // SIDE, section % SIDE
    far = column if mirror else last - column
    step = 1 if mirror else -1

    def any_of(spots):
        flag = jnp.bool_(False)
        for r, f in spots:
            flag = jnp.logical_or(flag, jnp.logical_and(row == r, far == f))
        return flag

    along = jnp.logical_or(jnp.logical_and(row < last, far < last), any_of([(3, 0)]))
    above = ((row + 1) % SIDE) * SIDE + column
    below = ((row + SIDE - 1) % SIDE) * SIDE + column
    edges = [
        (along, section + step),
        (any_of([(3, 0), (0, 0), (2, 2), (2, 3)]), above),
        (any_of([(3, 0)]), below),
    ]
    start = jnp.where(row == 1, 2, 1)
    depth = jnp.where(row == last, jnp.where(far < 2, far, far + 2), start + far)
    return edges, depth


def kernel(
    x_ref, gain_ref, win_hbm, wout_hbm, policy_ref, head_hbm, wanted_ref, out_ref,
    win_ref, wout_ref, head_ref,
    stream, partial, pieces, mine, twin_rows, leaving, final,
    logit_out, logit_in, pol_out, pol_in, stat_rows, stat_out, stat_in,
    load_sem, piece_send, piece_recv, twin_send, twin_recv, stream_send, stream_recv,
    final_send, final_recv, policy_send, logit_send, logit_recv, pol_send, pol_recv,
    stat_send, stat_recv,
):
    batches = stream.shape[0]
    width = stream.shape[2]
    units = wout_ref.shape[0]
    vocab_block = head_ref.shape[0]
    chunks = logit_out.shape[0]
    tensor_count = lax.axis_size("tensor")
    section_count = lax.axis_size("section")
    section = lax.axis_index("section")
    tensor = lax.axis_index("tensor")
    group = lax.axis_index("group")
    core = tensor % 2
    twin = tensor + 1 - 2 * core
    first_section = section == 0
    last_section = section == section_count - 1
    in_first = group == 0
    in_second = group == 1
    late_half = section >= section_count // 2
    entry = SIDE * (SIDE - 1)
    edges_a, depth_a = tree_edges(section, False)
    edges_b, depth_b = tree_edges(section, True)
    lag = depth_b + 1 - depth_a
    lag_a = jnp.where(in_first, jnp.maximum(-lag, 0), 0)
    lag_b = jnp.where(in_first, jnp.maximum(lag, 0), 0)
    lag_most = jnp.maximum(lag_a, lag_b)
    lag_limit = 6
    crossing_out = jnp.logical_and(last_section, in_second)

    loads = [
        pltpu.make_async_copy(win_hbm, win_ref, load_sem.at[0]),
        pltpu.make_async_copy(wout_hbm, wout_ref, load_sem.at[1]),
        pltpu.make_async_copy(head_hbm, head_ref, load_sem.at[2]),
    ]

    def own_block(source, target, place, sem):
        return pltpu.make_async_copy(
            source.at[block_at(place)],
            target.at[place // PER, pl.ds((place % PER) * BLOCK, BLOCK)],
            sem.at[place // PER],
        )

    places = batches * PER

    @pl.when(first_section)
    def _():
        def fetch(place, carry):
            own_block(x_ref, stream, place, stream_recv).start()
            return carry

        lax.fori_loop(0, places, fetch, 0)

    for load in loads:
        load.start()

    @pl.when(in_second)
    def _():
        def fetch(place, carry):
            pltpu.make_async_copy(
                policy_ref.at[block_at(place)],
                final.at[batches + place // PER, pl.ds((place % PER) * BLOCK, BLOCK)],
                final_recv.at[batches + place // PER],
            ).start()
            return carry

        lax.fori_loop(0, places, fetch, 0)

    stat_rows[...] = jnp.zeros_like(stat_rows)

    barrier = pltpu.get_barrier_semaphore()

    def greet(where):
        pl.semaphore_signal(barrier, 1, device_id=where, device_id_type=MESH)

    for offset in range(1, tensor_count):
        greet({"tensor": (tensor + offset) % tensor_count})
    for offset in range(section_count):
        greet({"section": (section + offset) % section_count, "group": 1 - group})

    @pl.when(in_first)
    def _():
        for offset in range(1, section_count):
            greet({"section": (section + offset) % section_count})

    @pl.when(jnp.logical_and(in_second, jnp.logical_not(first_section)))
    def _():
        greet({"section": section - 1})

    @pl.when(jnp.logical_and(in_second, jnp.logical_not(last_section)))
    def _():
        greet({"section": section + 1})

    neighbours = as_count(jnp.logical_not(first_section)) + as_count(jnp.logical_not(last_section))
    pl.semaphore_wait(
        barrier,
        tensor_count - 1 + section_count + jnp.where(in_first, section_count - 1, neighbours),
    )

    def policy_copy(place):
        return pltpu.make_async_remote_copy(
            src_ref=policy_ref.at[block_at(place)],
            dst_ref=final.at[place // PER, pl.ds((place % PER) * BLOCK, BLOCK)],
            send_sem=policy_send.at[place],
            recv_sem=final_recv.at[place // PER],
            device_id={"group": 1 - group},
            device_id_type=MESH,
        )

    def send_policy():
        def one(place, carry):
            policy_copy(place).start()
            return carry

        lax.fori_loop(0, places, one, 0)

    def piece_copy(batch, offset):
        target = (tensor + offset) % tensor_count
        return pltpu.make_async_remote_copy(
            src_ref=partial.at[batch, target % 2],
            dst_ref=pieces.at[batch, offset - 1],
            send_sem=piece_send.at[batch],
            recv_sem=piece_recv.at[batch],
            device_id={"tensor": target},
            device_id_type=MESH,
        )

    def twin_copy(batch):
        return pltpu.make_async_remote_copy(
            src_ref=mine.at[batch],
            dst_ref=twin_rows.at[batch],
            send_sem=twin_send.at[batch],
            recv_sem=twin_recv.at[batch],
            device_id={"tensor": twin},
            device_id_type=MESH,
        )

    def stream_copy(batch):
        return pltpu.make_async_remote_copy(
            src_ref=leaving.at[batch],
            dst_ref=stream.at[batch],
            send_sem=stream_send.at[batch],
            recv_sem=stream_recv.at[batch],
            device_id={"section": section + 1},
            device_id_type=MESH,
        )

    def final_copy(source, slot, edge, where):
        return pltpu.make_async_remote_copy(
            src_ref=source,
            dst_ref=final.at[slot],
            send_sem=final_send.at[slot, edge],
            recv_sem=final_recv.at[slot],
            device_id=where,
            device_id_type=MESH,
        )

    def crossing_copy(batch):
        return final_copy(leaving.at[batch], batches + batch, 0, {"section": entry, "group": 0})

    def all_bytes(ref, sem):
        return pltpu.make_async_copy(ref, ref, sem)

    def stage_a(batch):
        all_bytes(stream.at[batch], stream_recv.at[batch]).wait()
        values = stream[batch].astype(jnp.float32)
        squares = jnp.sum(values * values, axis=1, keepdims=True)
        scaled = (values * gain_ref[...]).astype(jnp.bfloat16)
        mixed = jnp.dot(scaled, win_ref[...], preferred_element_type=jnp.float32)
        squares = jnp.broadcast_to(squares, (ROWS, LANES))
        coarse = squares.astype(jnp.bfloat16).astype(jnp.float32)
        fine = squares - coarse
        for half in range(2):
            rows = slice(half * HALF, (half + 1) * HALF)
            partial[batch, half, :, :units] = jnp.concatenate(
                [mixed[rows, :units], mixed[rows, units:]], 0
            ).astype(jnp.bfloat16)
            partial[batch, half, :, units:] = jnp.concatenate(
                [coarse[rows], fine[rows]], 0
            ).astype(jnp.bfloat16)
        for offset in range(1, tensor_count):
            piece_copy(batch, offset).start()

    def stage_b(batch):
        all_bytes(pieces.at[batch], piece_recv.at[batch]).wait()
        total = partial[batch, core].astype(jnp.float32)
        for offset in range(1, tensor_count):
            total += pieces[batch, offset - 1].astype(jnp.float32)
        squares = total[:HALF, units:units + 1] + total[HALF:, units:units + 1]
        scale = lax.rsqrt(squares / (width * tensor_count) + epsilon)
        gate = total[:HALF, :units] * scale
        up = total[HALF:, :units] * scale
        mine[batch] = gate / (1.0 + jnp.exp(-gate)) * up
        twin_copy(batch).start()

    def stage_c(batch):
        twin_copy(batch).wait_recv()
        here, there = mine[batch], twin_rows[batch]
        hidden = jnp.concatenate(
            [jnp.where(core == 0, here, there), jnp.where(core == 0, there, here)], 0
        ).astype(jnp.bfloat16)
        update = jnp.dot(hidden, wout_ref[...], preferred_element_type=jnp.float32)
        leaving[batch] = (stream[batch].astype(jnp.float32) + update).astype(jnp.bfloat16)

        @pl.when(jnp.logical_not(last_section))
        def _():
            stream_copy(batch).start()

        @pl.when(jnp.logical_and(last_section, in_first))
        def _():
            final[batch] = leaving[batch]
            for edge, (_, target) in enumerate(edges_a):
                final_copy(leaving.at[batch], batch, edge, {"section": target}).start()

        @pl.when(crossing_out)
        def _():
            crossing_copy(batch).start()

    def relay():
        loads[0].wait()
        loads[1].wait()

        def step(index, carry):
            @pl.when(index < batches)
            def _():
                stage_a(index)

            @pl.when(index >= 1)
            def _():
                stage_b(index - 1)
                stage_c(index - 1)

            return carry

        lax.fori_loop(0, batches + 1, step, 0)

    def pass_on(slot, edges, root):
        @pl.when(jnp.logical_not(root))
        def _():
            all_bytes(final.at[slot], final_recv.at[slot]).wait()

            @pl.when(in_first)
            def _():
                for edge, (sends, target) in enumerate(edges):
                    @pl.when(sends)
                    def _(edge=edge, target=target):
                        final_copy(final.at[slot], slot, edge, {"section": target}).start()

    def logit_copy(chunk, offset):
        target = (tensor + offset) % tensor_count
        return pltpu.make_async_remote_copy(
            src_ref=logit_out.at[chunk, target],
            dst_ref=logit_in.at[chunk, offset - 1],
            send_sem=logit_send.at[chunk],
            recv_sem=logit_recv.at[chunk],
            device_id={"tensor": target},
            device_id_type=MESH,
        )

    def pol_copy(chunk):
        return pltpu.make_async_remote_copy(
            src_ref=pol_out.at[chunk],
            dst_ref=pol_in.at[chunk],
            send_sem=pol_send.at[chunk],
            recv_sem=pol_recv.at[chunk],
            device_id={"group": 1 - group},
            device_id_type=MESH,
        )

    per_chunk = CHUNK // ROWS

    def head_product(chunk):
        rows = jnp.concatenate(
            [
                final[pl.ds(chunk * per_chunk, per_chunk)].reshape(CHUNK, width),
                final[pl.ds(batches + chunk * per_chunk, per_chunk)].reshape(CHUNK, width),
            ],
            0,
        )
        logits = lax.dot_general(
            rows, head_ref[...], (((1,), (1,)), ((), ())), preferred_element_type=jnp.float32
        )
        logit_out[chunk] = logits.astype(jnp.bfloat16).reshape(
            tensor_count, 2 * CHUNK // tensor_count, vocab_block
        )
        for offset in range(1, tensor_count):
            logit_copy(chunk, offset).start()

    def head_total(chunk):
        all_bytes(logit_in.at[chunk], logit_recv.at[chunk]).wait()
        total = logit_out[chunk, tensor].astype(jnp.float32)
        for offset in range(1, tensor_count):
            total += logit_in[chunk, offset - 1].astype(jnp.float32)

        @pl.when(in_second)
        def _():
            pol_out[chunk] = total
            pol_copy(chunk).start()

        @pl.when(in_first)
        def _():
            pol_copy(chunk).wait_recv()
            pol = pol_in[chunk]
            rows = pl.ds(pl.multiple_of(chunk * BLOCK, BLOCK), BLOCK)
            ids = section * vocab_block + lax.broadcasted_iota(jnp.int32, pol.shape, 1)
            picked = jnp.where(ids == wanted_ref[rows, :1], pol, 0.0)
            peak_pol = jnp.max(pol, axis=1, keepdims=True)
            peak_ref = jnp.max(total, axis=1, keepdims=True)
            weights_pol = jnp.exp(pol - peak_pol)
            weights_ref = jnp.exp(total - peak_ref)
            stats = [
                peak_pol,
                peak_ref,
                jnp.sum(weights_pol, axis=1, keepdims=True),
                jnp.sum(weights_ref, axis=1, keepdims=True),
                jnp.sum(weights_pol * (pol - total), axis=1, keepdims=True),
                jnp.sum(picked, axis=1, keepdims=True),
            ]
            lane = lax.broadcasted_iota(jnp.int32, (BLOCK, LANES), 1)
            block = jnp.zeros((BLOCK, LANES), jnp.float32)
            for index, stat in enumerate(stats):
                block = jnp.where(lane == index, stat, block)
            stat_rows[rows, :] = block

    def head_work():
        loads[2].wait()

        def step(index, carry):
            @pl.when(jnp.logical_and(index >= lag_a, index < batches + lag_a))
            def _():
                pass_on(index - lag_a, edges_a, jnp.logical_and(last_section, in_first))

            @pl.when(jnp.logical_and(index >= lag_b, index < batches + lag_b))
            def _():
                pass_on(batches + index - lag_b, edges_b, jnp.bool_(False))

            done = index - lag_most + 1
            chunk = done // per_chunk - 1
            full = jnp.logical_and(done > 0, done % per_chunk == 0)

            @pl.when(jnp.logical_and(full, chunk < chunks))
            def _():
                head_product(chunk)

            @pl.when(jnp.logical_and(full, jnp.logical_and(chunk >= 1, chunk <= chunks)))
            def _():
                head_total(chunk - 1)

            return carry

        lax.fori_loop(0, batches + lag_limit + per_chunk, step, 0)

    def stat_copy(to_section, to_group):
        return pltpu.make_async_remote_copy(
            src_ref=stat_out,
            dst_ref=stat_in.at[section],
            send_sem=stat_send,
            recv_sem=stat_recv,
            device_id={"section": to_section, "group": to_group},
            device_id_type=MESH,
        )

    @pl.when(jnp.logical_and(in_first, late_half))
    def _():
        send_policy()

    head_phase = jnp.where(jnp.logical_and(in_second, late_half), 0, 2)

    def phase(index, carry):
        @pl.when(index == 1)
        def _():
            relay()

        @pl.when(jnp.logical_and(index == 2, jnp.logical_and(in_first, jnp.logical_not(late_half))))
        def _():
            send_policy()

        @pl.when(index == head_phase)
        def _():
            head_work()

        return carry

    lax.fori_loop(0, 3, phase, 0)

    @pl.when(in_first)
    def _():
        block = jnp.transpose(stat_rows[...])[:8]
        stat_out[...] = block
        stat_in[section] = block
        for offset in range(section_count):
            to_section = (section + offset) % section_count
            if offset:
                stat_copy(to_section, 0).start()
            stat_copy(to_section, 1).start()

    def drain(batch, carry):
        all_bytes(pieces.at[batch], piece_send.at[batch]).wait()
        twin_copy(batch).wait_send()

        @pl.when(jnp.logical_not(last_section))
        def _():
            stream_copy(batch).wait_send()

        @pl.when(in_first)
        def _():
            for first, edges in ((0, edges_a), (batches, edges_b)):
                for edge, (sends, target) in enumerate(edges):
                    @pl.when(sends)
                    def _(edge=edge, target=target, slot=first + batch):
                        final_copy(final.at[slot], slot, edge, {"section": target}).wait_send()

            for place in range(PER):
                policy_copy(batch * PER + place).wait_send()

        @pl.when(crossing_out)
        def _():
            crossing_copy(batch).wait_send()

        return carry

    lax.fori_loop(0, batches, drain, 0)

    def drain_logits(chunk, carry):
        all_bytes(logit_in.at[chunk], logit_send.at[chunk]).wait()

        @pl.when(in_second)
        def _():
            pol_copy(chunk).wait_send()

        return carry

    lax.fori_loop(0, chunks, drain_logits, 0)

    @pl.when(in_first)
    def _():
        all_bytes(stat_in.at[pl.ds(0, section_count - 1)], stat_recv).wait()

    @pl.when(in_second)
    def _():
        all_bytes(stat_in.at[pl.ds(0, section_count)], stat_recv).wait()

    peaks_pol = [stat_in[index, 0:1] for index in range(section_count)]
    peaks_ref = [stat_in[index, 1:2] for index in range(section_count)]
    peak_pol, peak_ref = peaks_pol[0], peaks_ref[0]
    for index in range(1, section_count):
        peak_pol = jnp.maximum(peak_pol, peaks_pol[index])
        peak_ref = jnp.maximum(peak_ref, peaks_ref[index])
    total_pol = jnp.zeros_like(peak_pol)
    total_ref = jnp.zeros_like(peak_pol)
    cross = jnp.zeros_like(peak_pol)
    chosen = jnp.zeros_like(peak_pol)
    for index in range(section_count):
        shift_pol = jnp.exp(peaks_pol[index] - peak_pol)
        shift_ref = jnp.exp(peaks_ref[index] - peak_ref)
        total_pol += shift_pol * stat_in[index, 2:3]
        total_ref += shift_ref * stat_in[index, 3:4]
        cross += shift_pol * stat_in[index, 4:5]
        chosen += stat_in[index, 5:6]
    lse_pol = peak_pol + jnp.log(total_pol)
    lse_ref = peak_ref + jnp.log(total_ref)
    out_ref[0:1] = cross / total_pol - lse_pol + lse_ref
    out_ref[1:2] = chosen - lse_pol
    out_ref[2:] = jnp.zeros((6, LANES), jnp.float32)

    @pl.when(in_first)
    def _():
        all_bytes(stat_in.at[pl.ds(0, 2 * section_count - 1)], stat_send).wait()


def token_terms(rows, gain, weight_in, weight_out, policy_rows, head, wanted):
    tensor_count = lax.axis_size("tensor")
    section_count = lax.axis_size("section")
    blocks, _, width = rows.shape
    batches = blocks // PER
    units = weight_out.shape[0]
    vocab_block = head.shape[0]
    chunks = blocks * BLOCK // CHUNK
    piece = (ROWS, units + LANES)
    logit = (BLOCK, vocab_block)
    dma = pltpu.SemaphoreType.DMA
    vmem = pl.BlockSpec(memory_space=pltpu.VMEM)
    hbm = pl.BlockSpec(memory_space=pl.ANY)
    bf16, f32 = jnp.bfloat16, jnp.float32
    return pl.pallas_call(
        kernel,
        out_shape=jax.ShapeDtypeStruct((8, LANES), f32),
        in_specs=[hbm, vmem, hbm, hbm, hbm, hbm, vmem],
        out_specs=vmem,
        scratch_shapes=[
            pltpu.VMEM(weight_in.shape, bf16),
            pltpu.VMEM(weight_out.shape, bf16),
            pltpu.VMEM(head.shape, bf16),
            pltpu.VMEM((batches, ROWS, width), bf16),
            pltpu.VMEM((batches, 2) + piece, bf16),
            pltpu.VMEM((batches, tensor_count - 1) + piece, bf16),
            pltpu.VMEM((batches, HALF, units), f32),
            pltpu.VMEM((batches, HALF, units), f32),
            pltpu.VMEM((batches, ROWS, width), bf16),
            pltpu.VMEM((2 * batches, ROWS, width), bf16),
            pltpu.VMEM((chunks, tensor_count) + logit, bf16),
            pltpu.VMEM((chunks, tensor_count - 1) + logit, bf16),
            pltpu.VMEM((chunks,) + logit, f32),
            pltpu.VMEM((chunks,) + logit, f32),
            pltpu.VMEM((LANES, LANES), f32),
            pltpu.VMEM((8, LANES), f32),
            pltpu.VMEM((2 * section_count, 8, LANES), f32),
            dma((3,)),
            dma((batches,)),
            dma((batches,)),
            dma((batches,)),
            dma((batches,)),
            dma((batches,)),
            dma((batches,)),
            dma((2 * batches, 3)),
            dma((2 * batches,)),
            dma((blocks,)),
            dma((chunks,)),
            dma((chunks,)),
            dma((chunks,)),
            dma((chunks,)),
            dma,
            dma,
        ],
        compiler_params=pltpu.CompilerParams(
            collective_id=0, has_side_effects=True, vmem_limit_bytes=48 * 1024 * 1024
        ),
        name="token_terms",
    )(rows, gain, weight_in, weight_out, policy_rows, head, wanted)


def advantages(rewards, prompt_ids):
    same = (prompt_ids[:, None] == prompt_ids[None, :]).astype(jnp.float32)
    counts = jnp.sum(same, axis=1)
    means = jnp.sum(same * rewards[None, :], axis=1) / counts
    spread = rewards[None, :] - means[:, None]
    variance = jnp.sum(same * spread * spread, axis=1) / counts
    return (rewards - means) / jnp.maximum(jnp.sqrt(variance), 1.0)


def shards(
    ref_input, norm_gain, w_in, w_out, policy_hidden, heads, sampled, live_mask, rewards, prompt_ids
):
    tensor_here = lax.axis_index("tensor")
    group_count = lax.axis_size("group")
    group_here = lax.axis_index("group")
    tokens = sampled.shape[0]
    per_tensor = tokens // lax.axis_size("tensor")
    local_rows = per_tensor // group_count
    width = ref_input.shape[3]
    wanted = lax.dynamic_slice_in_dim(sampled, tensor_here * per_tensor, per_tensor, 0)
    terms = token_terms(
        ref_input.reshape(-1, BLOCK, width),
        norm_gain,
        w_in[0],
        w_out[0],
        policy_hidden.reshape(-1, BLOCK, width),
        heads[0],
        jnp.broadcast_to(wanted[:, None], (per_tensor, LANES)),
    )
    terms = lax.dynamic_slice_in_dim(terms[:2], group_here * local_rows, local_rows, 1)
    token_kl, log_prob = terms[0], terms[1]
    row_start = (tensor_here * group_count + group_here) * local_rows
    token_adv = lax.dynamic_slice_in_dim(
        jnp.repeat(advantages(rewards, prompt_ids), RLEN), row_start, local_rows, 0
    )
    live = lax.dynamic_slice_in_dim(live_mask, row_start, local_rows, 0).astype(jnp.float32)
    token_loss = live * (penalty * token_kl - token_adv * log_prob) / RLEN
    return (token_kl, token_loss)


def solution(mesh):
    in_specs = (
        P("group", None, None, "tensor"),
        P("section", "tensor"),
        P("section", "tensor", None),
        P("section", None, "tensor"),
        P("group", "tensor"),
        P("group", "section", "tensor"),
        P(),
        P(),
        P(),
        P(),
    )
    out_specs = (P(("tensor", "group")), P(("tensor", "group")))
    return jax.shard_map(shards, mesh=mesh, in_specs=in_specs, out_specs=out_specs, check_vma=False)
```

```python
import jax
import jax.numpy as jnp
from jax import lax
from jax.experimental import pallas as pl
from jax.experimental.pallas import tpu as pltpu
from jax.sharding import PartitionSpec as P

RLEN = 64
SIDE = 4
BLOCK = 16
ROWS = 32
HALF = ROWS // 2
PER = ROWS // BLOCK
CHUNK = 64
LANES = 128

epsilon = 1e-05
penalty = 0.04
MESH = pl.DeviceIdType.MESH


def as_count(flag):
    return jnp.where(flag, 1, 0).astype(jnp.int32)


def block_at(place):
    return (place % SIDE) * SIDE + place // SIDE


def tree_edges(section, mirror):
    last = SIDE - 1
    row, column = section // SIDE, section % SIDE
    far = column if mirror else last - column
    step = 1 if mirror else -1

    def any_of(spots):
        flag = jnp.bool_(False)
        for r, f in spots:
            flag = jnp.logical_or(flag, jnp.logical_and(row == r, far == f))
        return flag

    along = jnp.logical_or(jnp.logical_and(row < last, far < last), any_of([(3, 0)]))
    above = ((row + 1) % SIDE) * SIDE + column
    below = ((row + SIDE - 1) % SIDE) * SIDE + column
    edges = [
        (along, section + step),
        (any_of([(3, 0), (0, 0), (2, 2), (2, 3)]), above),
        (any_of([(3, 0)]), below),
    ]
    start = jnp.where(row == 1, 2, 1)
    depth = jnp.where(row == last, jnp.where(far < 2, far, far + 2), start + far)
    return edges, depth


def kernel(
    x_ref, gain_ref, win_hbm, wout_hbm, policy_ref, head_hbm, wanted_ref, out_ref,
    win_ref, wout_ref, head_ref,
    stream, partial, pieces, mine, twin_rows, leaving, final,
    logit_out, logit_in, pol_out, pol_in, stat_rows, stat_out, stat_in,
    load_sem, piece_send, piece_recv, twin_send, twin_recv, stream_send, stream_recv,
    final_send, final_recv, policy_send, logit_send, logit_recv, pol_send, pol_recv,
    stat_send, stat_recv,
):
    batches = stream.shape[0]
    width = stream.shape[2]
    units = wout_ref.shape[0]
    vocab_block = head_ref.shape[0]
    chunks = logit_out.shape[0]
    tensor_count = lax.axis_size("tensor")
    section_count = lax.axis_size("section")
    section = lax.axis_index("section")
    tensor = lax.axis_index("tensor")
    group = lax.axis_index("group")
    core = tensor % 2
    twin = tensor + 1 - 2 * core
    first_section = section == 0
    last_section = section == section_count - 1
    in_first = group == 0
    in_second = group == 1
    late_half = section >= section_count // 2
    entry = SIDE * (SIDE - 1)
    edges_a, depth_a = tree_edges(section, False)
    edges_b, depth_b = tree_edges(section, True)
    lag = depth_b + 1 - depth_a
    lag_a = jnp.where(in_first, jnp.maximum(-lag, 0), 0)
    lag_b = jnp.where(in_first, jnp.maximum(lag, 0), 0)
    lag_most = jnp.maximum(lag_a, lag_b)
    lag_limit = 6
    crossing_out = jnp.logical_and(last_section, in_second)
    policy_source = jnp.logical_and(in_first, late_half)
    policy_passes = jnp.logical_and(in_second, late_half)
    across = (SIDE - 1 - section // SIDE) * SIDE + section % SIDE

    loads = [
        pltpu.make_async_copy(win_hbm, win_ref, load_sem.at[0]),
        pltpu.make_async_copy(wout_hbm, wout_ref, load_sem.at[1]),
        pltpu.make_async_copy(head_hbm, head_ref, load_sem.at[2]),
    ]

    def own_block(source, target, place, sem):
        return pltpu.make_async_copy(
            source.at[block_at(place)],
            target.at[place // PER, pl.ds((place % PER) * BLOCK, BLOCK)],
            sem.at[place // PER],
        )

    places = batches * PER

    @pl.when(first_section)
    def _():
        def fetch(place, carry):
            own_block(x_ref, stream, place, stream_recv).start()
            return carry

        lax.fori_loop(0, places, fetch, 0)

    for load in loads:
        load.start()

    @pl.when(in_second)
    def _():
        def fetch(place, carry):
            pltpu.make_async_copy(
                policy_ref.at[block_at(place)],
                final.at[batches + place // PER, pl.ds((place % PER) * BLOCK, BLOCK)],
                final_recv.at[batches + place // PER],
            ).start()
            return carry

        lax.fori_loop(0, places, fetch, 0)

    stat_rows[...] = jnp.zeros_like(stat_rows)

    barrier = pltpu.get_barrier_semaphore()

    def greet(where):
        pl.semaphore_signal(barrier, 1, device_id=where, device_id_type=MESH)

    for offset in range(1, tensor_count):
        greet({"tensor": (tensor + offset) % tensor_count})
    for offset in range(section_count):
        greet({"section": (section + offset) % section_count, "group": 1 - group})

    @pl.when(in_first)
    def _():
        for offset in range(1, section_count):
            greet({"section": (section + offset) % section_count})

    @pl.when(in_second)
    def _():
        greet({"section": across})

    @pl.when(jnp.logical_and(in_second, jnp.logical_not(first_section)))
    def _():
        greet({"section": section - 1})

    @pl.when(jnp.logical_and(in_second, jnp.logical_not(last_section)))
    def _():
        greet({"section": section + 1})

    neighbours = as_count(jnp.logical_not(first_section)) + as_count(jnp.logical_not(last_section))
    pl.semaphore_wait(
        barrier,
        tensor_count - 1 + section_count + jnp.where(in_first, section_count - 1, neighbours + 1),
    )

    def policy_copy(place):
        return pltpu.make_async_remote_copy(
            src_ref=policy_ref.at[block_at(place)],
            dst_ref=final.at[place // PER, pl.ds((place % PER) * BLOCK, BLOCK)],
            send_sem=policy_send.at[place],
            recv_sem=final_recv.at[place // PER],
            device_id={"group": 1 - group},
            device_id_type=MESH,
        )

    def send_policy():
        def one(place, carry):
            policy_copy(place).start()
            return carry

        lax.fori_loop(0, places, one, 0)

    def piece_copy(batch, offset):
        target = (tensor + offset) % tensor_count
        return pltpu.make_async_remote_copy(
            src_ref=partial.at[batch, target % 2],
            dst_ref=pieces.at[batch, offset - 1],
            send_sem=piece_send.at[batch],
            recv_sem=piece_recv.at[batch],
            device_id={"tensor": target},
            device_id_type=MESH,
        )

    def twin_copy(batch):
        return pltpu.make_async_remote_copy(
            src_ref=mine.at[batch],
            dst_ref=twin_rows.at[batch],
            send_sem=twin_send.at[batch],
            recv_sem=twin_recv.at[batch],
            device_id={"tensor": twin},
            device_id_type=MESH,
        )

    def stream_copy(batch):
        return pltpu.make_async_remote_copy(
            src_ref=leaving.at[batch],
            dst_ref=stream.at[batch],
            send_sem=stream_send.at[batch],
            recv_sem=stream_recv.at[batch],
            device_id={"section": section + 1},
            device_id_type=MESH,
        )

    def final_copy(source, slot, edge, where):
        return pltpu.make_async_remote_copy(
            src_ref=source,
            dst_ref=final.at[slot],
            send_sem=final_send.at[slot, edge],
            recv_sem=final_recv.at[slot],
            device_id=where,
            device_id_type=MESH,
        )

    def crossing_copy(batch):
        return final_copy(leaving.at[batch], batches + batch, 0, {"section": entry, "group": 0})

    def all_bytes(ref, sem):
        return pltpu.make_async_copy(ref, ref, sem)

    def stage_a(batch):
        all_bytes(stream.at[batch], stream_recv.at[batch]).wait()
        values = stream[batch].astype(jnp.float32)
        squares = jnp.sum(values * values, axis=1, keepdims=True)
        scaled = (values * gain_ref[...]).astype(jnp.bfloat16)
        mixed = jnp.dot(scaled, win_ref[...], preferred_element_type=jnp.float32)
        squares = jnp.broadcast_to(squares, (ROWS, LANES))
        coarse = squares.astype(jnp.bfloat16).astype(jnp.float32)
        fine = squares - coarse
        for half in range(2):
            rows = slice(half * HALF, (half + 1) * HALF)
            partial[batch, half, :, :units] = jnp.concatenate(
                [mixed[rows, :units], mixed[rows, units:]], 0
            ).astype(jnp.bfloat16)
            partial[batch, half, :, units:] = jnp.concatenate(
                [coarse[rows], fine[rows]], 0
            ).astype(jnp.bfloat16)
        for offset in range(1, tensor_count):
            piece_copy(batch, offset).start()

    def stage_b(batch):
        all_bytes(pieces.at[batch], piece_recv.at[batch]).wait()
        total = partial[batch, core].astype(jnp.float32)
        for offset in range(1, tensor_count):
            total += pieces[batch, offset - 1].astype(jnp.float32)
        squares = total[:HALF, units:units + 1] + total[HALF:, units:units + 1]
        scale = lax.rsqrt(squares / (width * tensor_count) + epsilon)
        gate = total[:HALF, :units] * scale
        up = total[HALF:, :units] * scale
        mine[batch] = gate / (1.0 + jnp.exp(-gate)) * up
        twin_copy(batch).start()

    def stage_c(batch):
        twin_copy(batch).wait_recv()
        here, there = mine[batch], twin_rows[batch]
        hidden = jnp.concatenate(
            [jnp.where(core == 0, here, there), jnp.where(core == 0, there, here)], 0
        ).astype(jnp.bfloat16)
        update = jnp.dot(hidden, wout_ref[...], preferred_element_type=jnp.float32)
        leaving[batch] = (stream[batch].astype(jnp.float32) + update).astype(jnp.bfloat16)

        @pl.when(jnp.logical_not(last_section))
        def _():
            stream_copy(batch).start()

        @pl.when(jnp.logical_and(last_section, in_first))
        def _():
            final[batch] = leaving[batch]
            for edge, (_, target) in enumerate(edges_a):
                final_copy(leaving.at[batch], batch, edge, {"section": target}).start()

        @pl.when(crossing_out)
        def _():
            crossing_copy(batch).start()

    def relay():
        loads[0].wait()
        loads[1].wait()

        def step(index, carry):
            @pl.when(index < batches)
            def _():
                stage_a(index)

            @pl.when(index >= 1)
            def _():
                stage_b(index - 1)
                stage_c(index - 1)

            return carry

        lax.fori_loop(0, batches + 1, step, 0)

    def pass_on(slot, edges, root):
        @pl.when(jnp.logical_not(root))
        def _():
            all_bytes(final.at[slot], final_recv.at[slot]).wait()

            @pl.when(in_first)
            def _():
                for edge, (sends, target) in enumerate(edges):
                    @pl.when(sends)
                    def _(edge=edge, target=target):
                        final_copy(final.at[slot], slot, edge, {"section": target}).start()

            @pl.when(jnp.logical_and(policy_passes, slot < batches))
            def _():
                final_copy(final.at[slot], slot, 0, {"section": across}).start()

    def logit_copy(chunk, offset):
        target = (tensor + offset) % tensor_count
        return pltpu.make_async_remote_copy(
            src_ref=logit_out.at[chunk, target],
            dst_ref=logit_in.at[chunk, offset - 1],
            send_sem=logit_send.at[chunk],
            recv_sem=logit_recv.at[chunk],
            device_id={"tensor": target},
            device_id_type=MESH,
        )

    def pol_copy(chunk):
        return pltpu.make_async_remote_copy(
            src_ref=pol_out.at[chunk],
            dst_ref=pol_in.at[chunk],
            send_sem=pol_send.at[chunk],
            recv_sem=pol_recv.at[chunk],
            device_id={"group": 1 - group},
            device_id_type=MESH,
        )

    per_chunk = CHUNK // ROWS

    def head_product(chunk):
        rows = jnp.concatenate(
            [
                final[pl.ds(chunk * per_chunk, per_chunk)].reshape(CHUNK, width),
                final[pl.ds(batches + chunk * per_chunk, per_chunk)].reshape(CHUNK, width),
            ],
            0,
        )
        logits = lax.dot_general(
            rows, head_ref[...], (((1,), (1,)), ((), ())), preferred_element_type=jnp.float32
        )
        logit_out[chunk] = logits.astype(jnp.bfloat16).reshape(
            tensor_count, 2 * CHUNK // tensor_count, vocab_block
        )
        for offset in range(1, tensor_count):
            logit_copy(chunk, offset).start()

    def head_total(chunk):
        all_bytes(logit_in.at[chunk], logit_recv.at[chunk]).wait()
        total = logit_out[chunk, tensor].astype(jnp.float32)
        for offset in range(1, tensor_count):
            total += logit_in[chunk, offset - 1].astype(jnp.float32)

        @pl.when(in_second)
        def _():
            pol_out[chunk] = total
            pol_copy(chunk).start()

        @pl.when(in_first)
        def _():
            pol_copy(chunk).wait_recv()
            pol = pol_in[chunk]
            rows = pl.ds(pl.multiple_of(chunk * BLOCK, BLOCK), BLOCK)
            ids = section * vocab_block + lax.broadcasted_iota(jnp.int32, pol.shape, 1)
            picked = jnp.where(ids == wanted_ref[rows, :1], pol, 0.0)
            peak_pol = jnp.max(pol, axis=1, keepdims=True)
            peak_ref = jnp.max(total, axis=1, keepdims=True)
            weights_pol = jnp.exp(pol - peak_pol)
            weights_ref = jnp.exp(total - peak_ref)
            stats = [
                peak_pol,
                peak_ref,
                jnp.sum(weights_pol, axis=1, keepdims=True),
                jnp.sum(weights_ref, axis=1, keepdims=True),
                jnp.sum(weights_pol * (pol - total), axis=1, keepdims=True),
                jnp.sum(picked, axis=1, keepdims=True),
            ]
            lane = lax.broadcasted_iota(jnp.int32, (BLOCK, LANES), 1)
            block = jnp.zeros((BLOCK, LANES), jnp.float32)
            for index, stat in enumerate(stats):
                block = jnp.where(lane == index, stat, block)
            stat_rows[rows, :] = block

    def head_work():
        loads[2].wait()

        def step(index, carry):
            @pl.when(jnp.logical_and(index >= lag_a, index < batches + lag_a))
            def _():
                pass_on(index - lag_a, edges_a, jnp.logical_and(last_section, in_first))

            @pl.when(jnp.logical_and(index >= lag_b, index < batches + lag_b))
            def _():
                pass_on(batches + index - lag_b, edges_b, jnp.bool_(False))

            done = index - lag_most + 1
            chunk = done // per_chunk - 1
            full = jnp.logical_and(done > 0, done % per_chunk == 0)

            @pl.when(jnp.logical_and(full, chunk < chunks))
            def _():
                head_product(chunk)

            @pl.when(jnp.logical_and(full, jnp.logical_and(chunk >= 1, chunk <= chunks)))
            def _():
                head_total(chunk - 1)

            return carry

        lax.fori_loop(0, batches + lag_limit + per_chunk, step, 0)

    def stat_copy(to_section, to_group):
        return pltpu.make_async_remote_copy(
            src_ref=stat_out,
            dst_ref=stat_in.at[section],
            send_sem=stat_send,
            recv_sem=stat_recv,
            device_id={"section": to_section, "group": to_group},
            device_id_type=MESH,
        )

    @pl.when(policy_source)
    def _():
        send_policy()

    head_phase = jnp.where(policy_passes, 0, 2)

    def phase(index, carry):
        @pl.when(index == 1)
        def _():
            relay()

        @pl.when(index == head_phase)
        def _():
            head_work()

        return carry

    lax.fori_loop(0, 3, phase, 0)

    @pl.when(in_first)
    def _():
        block = jnp.transpose(stat_rows[...])[:8]
        stat_out[...] = block
        stat_in[section] = block
        for offset in range(section_count):
            to_section = (section + offset) % section_count
            if offset:
                stat_copy(to_section, 0).start()
            stat_copy(to_section, 1).start()

    def drain(batch, carry):
        all_bytes(pieces.at[batch], piece_send.at[batch]).wait()
        twin_copy(batch).wait_send()

        @pl.when(jnp.logical_not(last_section))
        def _():
            stream_copy(batch).wait_send()

        @pl.when(in_first)
        def _():
            for first, edges in ((0, edges_a), (batches, edges_b)):
                for edge, (sends, target) in enumerate(edges):
                    @pl.when(sends)
                    def _(edge=edge, target=target, slot=first + batch):
                        final_copy(final.at[slot], slot, edge, {"section": target}).wait_send()

        @pl.when(policy_source)
        def _():
            for place in range(PER):
                policy_copy(batch * PER + place).wait_send()

        @pl.when(policy_passes)
        def _():
            final_copy(final.at[batch], batch, 0, {"section": across}).wait_send()

        @pl.when(crossing_out)
        def _():
            crossing_copy(batch).wait_send()

        return carry

    lax.fori_loop(0, batches, drain, 0)

    def drain_logits(chunk, carry):
        all_bytes(logit_in.at[chunk], logit_send.at[chunk]).wait()

        @pl.when(in_second)
        def _():
            pol_copy(chunk).wait_send()

        return carry

    lax.fori_loop(0, chunks, drain_logits, 0)

    @pl.when(in_first)
    def _():
        all_bytes(stat_in.at[pl.ds(0, section_count - 1)], stat_recv).wait()

    @pl.when(in_second)
    def _():
        all_bytes(stat_in.at[pl.ds(0, section_count)], stat_recv).wait()

    peaks_pol = [stat_in[index, 0:1] for index in range(section_count)]
    peaks_ref = [stat_in[index, 1:2] for index in range(section_count)]
    peak_pol, peak_ref = peaks_pol[0], peaks_ref[0]
    for index in range(1, section_count):
        peak_pol = jnp.maximum(peak_pol, peaks_pol[index])
        peak_ref = jnp.maximum(peak_ref, peaks_ref[index])
    total_pol = jnp.zeros_like(peak_pol)
    total_ref = jnp.zeros_like(peak_pol)
    cross = jnp.zeros_like(peak_pol)
    chosen = jnp.zeros_like(peak_pol)
    for index in range(section_count):
        shift_pol = jnp.exp(peaks_pol[index] - peak_pol)
        shift_ref = jnp.exp(peaks_ref[index] - peak_ref)
        total_pol += shift_pol * stat_in[index, 2:3]
        total_ref += shift_ref * stat_in[index, 3:4]
        cross += shift_pol * stat_in[index, 4:5]
        chosen += stat_in[index, 5:6]
    lse_pol = peak_pol + jnp.log(total_pol)
    lse_ref = peak_ref + jnp.log(total_ref)
    out_ref[0:1] = cross / total_pol - lse_pol + lse_ref
    out_ref[1:2] = chosen - lse_pol
    out_ref[2:] = jnp.zeros((6, LANES), jnp.float32)

    @pl.when(in_first)
    def _():
        all_bytes(stat_in.at[pl.ds(0, 2 * section_count - 1)], stat_send).wait()


def token_terms(rows, gain, weight_in, weight_out, policy_rows, head, wanted):
    tensor_count = lax.axis_size("tensor")
    section_count = lax.axis_size("section")
    blocks, _, width = rows.shape
    batches = blocks // PER
    units = weight_out.shape[0]
    vocab_block = head.shape[0]
    chunks = blocks * BLOCK // CHUNK
    piece = (ROWS, units + LANES)
    logit = (BLOCK, vocab_block)
    dma = pltpu.SemaphoreType.DMA
    vmem = pl.BlockSpec(memory_space=pltpu.VMEM)
    hbm = pl.BlockSpec(memory_space=pltpu.HBM)
    bf16, f32 = jnp.bfloat16, jnp.float32
    return pl.pallas_call(
        kernel,
        out_shape=jax.ShapeDtypeStruct((8, LANES), f32),
        in_specs=[hbm, vmem, hbm, hbm, hbm, hbm, vmem],
        out_specs=vmem,
        scratch_shapes=[
            pltpu.VMEM(weight_in.shape, bf16),
            pltpu.VMEM(weight_out.shape, bf16),
            pltpu.VMEM(head.shape, bf16),
            pltpu.VMEM((batches, ROWS, width), bf16),
            pltpu.VMEM((batches, 2) + piece, bf16),
            pltpu.VMEM((batches, tensor_count - 1) + piece, bf16),
            pltpu.VMEM((batches, HALF, units), f32),
            pltpu.VMEM((batches, HALF, units), f32),
            pltpu.VMEM((batches, ROWS, width), bf16),
            pltpu.VMEM((2 * batches, ROWS, width), bf16),
            pltpu.VMEM((chunks, tensor_count) + logit, bf16),
            pltpu.VMEM((chunks, tensor_count - 1) + logit, bf16),
            pltpu.VMEM((chunks,) + logit, f32),
            pltpu.VMEM((chunks,) + logit, f32),
            pltpu.VMEM((LANES, LANES), f32),
            pltpu.VMEM((8, LANES), f32),
            pltpu.VMEM((2 * section_count, 8, LANES), f32),
            dma((3,)),
            dma((batches,)),
            dma((batches,)),
            dma((batches,)),
            dma((batches,)),
            dma((batches,)),
            dma((batches,)),
            dma((2 * batches, 3)),
            dma((2 * batches,)),
            dma((blocks,)),
            dma((chunks,)),
            dma((chunks,)),
            dma((chunks,)),
            dma((chunks,)),
            dma,
            dma,
        ],
        compiler_params=pltpu.CompilerParams(
            collective_id=0, has_side_effects=True, vmem_limit_bytes=48 * 1024 * 1024
        ),
        name="token_terms",
    )(rows, gain, weight_in, weight_out, policy_rows, head, wanted)


def advantages(rewards, prompt_ids):
    same = (prompt_ids[:, None] == prompt_ids[None, :]).astype(jnp.float32)
    counts = jnp.sum(same, axis=1)
    means = jnp.sum(same * rewards[None, :], axis=1) / counts
    spread = rewards[None, :] - means[:, None]
    variance = jnp.sum(same * spread * spread, axis=1) / counts
    return (rewards - means) / jnp.maximum(jnp.sqrt(variance), 1.0)


def shards(
    ref_input, norm_gain, w_in, w_out, policy_hidden, heads, sampled, live_mask, rewards, prompt_ids
):
    tensor_here = lax.axis_index("tensor")
    group_count = lax.axis_size("group")
    group_here = lax.axis_index("group")
    tokens = sampled.shape[0]
    per_tensor = tokens // lax.axis_size("tensor")
    local_rows = per_tensor // group_count
    width = ref_input.shape[3]
    wanted = lax.dynamic_slice_in_dim(sampled, tensor_here * per_tensor, per_tensor, 0)
    terms = token_terms(
        ref_input.reshape(-1, BLOCK, width),
        norm_gain,
        w_in[0],
        w_out[0],
        policy_hidden.reshape(-1, BLOCK, width),
        heads[0],
        jnp.broadcast_to(wanted[:, None], (per_tensor, LANES)),
    )
    terms = lax.dynamic_slice_in_dim(terms[:2], group_here * local_rows, local_rows, 1)
    token_kl, log_prob = terms[0], terms[1]
    row_start = (tensor_here * group_count + group_here) * local_rows
    token_adv = lax.dynamic_slice_in_dim(
        jnp.repeat(advantages(rewards, prompt_ids), RLEN), row_start, local_rows, 0
    )
    live = lax.dynamic_slice_in_dim(live_mask, row_start, local_rows, 0).astype(jnp.float32)
    token_loss = live * (penalty * token_kl - token_adv * log_prob) / RLEN
    return (token_kl, token_loss)


def solution(mesh):
    in_specs = (
        P("group", None, None, "tensor"),
        P("section", "tensor"),
        P("section", "tensor", None),
        P("section", None, "tensor"),
        P("group", "tensor"),
        P("group", "section", "tensor"),
        P(),
        P(),
        P(),
        P(),
    )
    out_specs = (P(("tensor", "group")), P(("tensor", "group")))
    return jax.shard_map(shards, mesh=mesh, in_specs=in_specs, out_specs=out_specs, check_vma=False)
```

```python
import jax
import jax.numpy as jnp
from jax import lax
from jax.experimental import pallas as pl
from jax.experimental.pallas import tpu as pltpu
from jax.sharding import PartitionSpec as P

RLEN = 64
SIDE = 4
BLOCK = 16
ROWS = 32
HALF = ROWS // 2
PER = ROWS // BLOCK
CHUNK = 64
LANES = 128

epsilon = 1e-05
penalty = 0.04
MESH = pl.DeviceIdType.MESH


def as_count(flag):
    return jnp.where(flag, 1, 0).astype(jnp.int32)


def block_at(place):
    return (place % SIDE) * SIDE + place // SIDE


def tree_edges(section, mirror):
    last = SIDE - 1
    row, column = section // SIDE, section % SIDE
    far = column if mirror else last - column
    step = 1 if mirror else -1

    def any_of(spots):
        flag = jnp.bool_(False)
        for r, f in spots:
            flag = jnp.logical_or(flag, jnp.logical_and(row == r, far == f))
        return flag

    along = jnp.logical_or(jnp.logical_and(row < last, far < last), any_of([(3, 0)]))
    above = ((row + 1) % SIDE) * SIDE + column
    below = ((row + SIDE - 1) % SIDE) * SIDE + column
    edges = [
        (along, section + step),
        (any_of([(3, 0), (0, 0), (2, 2), (2, 3)]), above),
        (any_of([(3, 0)]), below),
    ]
    start = jnp.where(row == 1, 2, 1)
    depth = jnp.where(row == last, jnp.where(far < 2, far, far + 2), start + far)
    return edges, depth


def kernel(
    x_ref, gain_hbm, win_hbm, wout_hbm, policy_ref, head_hbm, sampled_hbm, out_ref,
    gain_ref, win_ref, wout_ref, before_ref, head_ref, sampled_ref,
    blend_out, blend_in, blend,
    stream, partial, pieces, square_out, square_in, mine, arrived, twin_rows, leaving, ending, final,
    logit_out, logit_in, pol_out, pol_in, stat_rows, stat_out, stat_in,
    load_sem, weight_send, weight_recv, blend_send, blend_recv,
    piece_send, piece_recv, square_send, square_recv, unit_send, unit_recv,
    twin_send, twin_recv, stream_send, stream_recv,
    final_send, final_recv, policy_send, logit_send, logit_recv, pol_send, pol_recv,
    stat_send, stat_recv,
):
    batches = stream.shape[0]
    width = stream.shape[2]
    units = wout_ref.shape[0]
    vocab_block = head_ref.shape[0]
    chunks = logit_out.shape[0]
    tensor_count = lax.axis_size("tensor")
    section_count = lax.axis_size("section")
    section = lax.axis_index("section")
    tensor = lax.axis_index("tensor")
    group = lax.axis_index("group")
    core = tensor % 2
    twin = tensor + 1 - 2 * core
    first_section = section == 0
    last_section = section == section_count - 1
    in_first = group == 0
    in_second = group == 1
    late_half = section >= section_count // 2
    entry = SIDE * (SIDE - 1)
    edges_a, depth_a = tree_edges(section, False)
    edges_b, depth_b = tree_edges(section, True)
    lag = depth_b + 1 - depth_a
    lag_a = jnp.where(in_first, jnp.maximum(-lag, 0), 0)
    lag_b = jnp.where(in_first, jnp.maximum(lag, 0), 0)
    lag_most = jnp.maximum(lag_a, lag_b)
    lag_limit = 6
    crossing_out = jnp.logical_and(last_section, in_second)
    policy_source = jnp.logical_and(in_first, late_half)
    policy_passes = jnp.logical_and(in_second, late_half)
    across = (SIDE - 1 - section // SIDE) * SIDE + section % SIDE

    loads = [
        pltpu.make_async_copy(gain_hbm, gain_ref, load_sem.at[0]),
        pltpu.make_async_copy(win_hbm, win_ref, load_sem.at[1]),
        pltpu.make_async_copy(wout_hbm, wout_ref, load_sem.at[2]),
        pltpu.make_async_copy(head_hbm, head_ref, load_sem.at[3]),
        pltpu.make_async_copy(sampled_hbm, sampled_ref, load_sem.at[4]),
    ]

    def own_block(source, target, place, sem):
        return pltpu.make_async_copy(
            source.at[block_at(place)],
            target.at[place // PER, pl.ds((place % PER) * BLOCK, BLOCK)],
            sem.at[place // PER],
        )

    places = batches * PER

    @pl.when(section < 2)
    def _():
        def fetch(place, carry):
            own_block(x_ref, stream, place, stream_recv).start()
            return carry

        lax.fori_loop(0, places, fetch, 0)

    for load in loads:
        load.start()

    @pl.when(in_second)
    def _():
        def fetch(place, carry):
            pltpu.make_async_copy(
                policy_ref.at[block_at(place)],
                final.at[batches + place // PER, pl.ds((place % PER) * BLOCK, BLOCK)],
                final_recv.at[batches + place // PER],
            ).start()
            return carry

        lax.fori_loop(0, places, fetch, 0)

    barrier = pltpu.get_barrier_semaphore()

    def greet(where):
        pl.semaphore_signal(barrier, 1, device_id=where, device_id_type=MESH)

    for offset in range(1, tensor_count):
        greet({"tensor": (tensor + offset) % tensor_count})
    for offset in range(section_count):
        greet({"section": (section + offset) % section_count, "group": 1 - group})

    @pl.when(in_first)
    def _():
        for offset in range(1, section_count):
            greet({"section": (section + offset) % section_count})

    @pl.when(in_second)
    def _():
        greet({"section": across})

    @pl.when(jnp.logical_and(in_second, jnp.logical_not(first_section)))
    def _():
        greet({"section": section - 1})

    @pl.when(jnp.logical_and(in_second, jnp.logical_not(last_section)))
    def _():
        greet({"section": section + 1})

    @pl.when(jnp.logical_not(first_section))
    def _():
        greet({"section": section - 1, "tensor": twin})

    @pl.when(jnp.logical_not(last_section))
    def _():
        greet({"section": section + 1, "tensor": twin})

    neighbours = as_count(jnp.logical_not(first_section)) + as_count(jnp.logical_not(last_section))
    pl.semaphore_wait(
        barrier,
        tensor_count - 1 + section_count + neighbours + jnp.where(in_first, section_count - 1, neighbours + 1),
    )

    def all_bytes(ref, sem):
        return pltpu.make_async_copy(ref, ref, sem)

    def to_peer(source, target, send_sem, recv_sem, offset):
        return pltpu.make_async_remote_copy(
            src_ref=source,
            dst_ref=target,
            send_sem=send_sem,
            recv_sem=recv_sem,
            device_id={"tensor": (tensor + offset) % tensor_count},
            device_id_type=MESH,
        )

    weight_copy = pltpu.make_async_remote_copy(
        src_ref=wout_hbm,
        dst_ref=before_ref,
        send_sem=weight_send,
        recv_sem=weight_recv,
        device_id={"section": section + 1},
        device_id_type=MESH,
    )

    @pl.when(jnp.logical_not(last_section))
    def _():
        weight_copy.start()

    def policy_copy(place):
        return pltpu.make_async_remote_copy(
            src_ref=policy_ref.at[block_at(place)],
            dst_ref=final.at[place // PER, pl.ds((place % PER) * BLOCK, BLOCK)],
            send_sem=policy_send.at[place],
            recv_sem=final_recv.at[place // PER],
            device_id={"group": 1 - group},
            device_id_type=MESH,
        )

    def send_policy():
        def one(place, carry):
            policy_copy(place).start()
            return carry

        lax.fori_loop(0, places, one, 0)

    def unit_copy(batch, where):
        return pltpu.make_async_remote_copy(
            src_ref=mine.at[batch],
            dst_ref=arrived.at[batch, core],
            send_sem=unit_send.at[batch],
            recv_sem=unit_recv.at[batch, core],
            device_id={"section": section + 1, "tensor": where},
            device_id_type=MESH,
        )

    def twin_copy(batch):
        return pltpu.make_async_remote_copy(
            src_ref=mine.at[batch],
            dst_ref=twin_rows.at[batch],
            send_sem=twin_send.at[batch],
            recv_sem=twin_recv.at[batch],
            device_id={"tensor": twin},
            device_id_type=MESH,
        )

    def stream_copy(batch):
        return pltpu.make_async_remote_copy(
            src_ref=leaving.at[batch],
            dst_ref=stream.at[batch],
            send_sem=stream_send.at[batch],
            recv_sem=stream_recv.at[batch],
            device_id={"section": section + 1},
            device_id_type=MESH,
        )

    def final_copy(source, slot, edge, where):
        return pltpu.make_async_remote_copy(
            src_ref=source,
            dst_ref=final.at[slot],
            send_sem=final_send.at[slot, edge],
            recv_sem=final_recv.at[slot],
            device_id=where,
            device_id_type=MESH,
        )

    def crossing_copy(batch):
        return final_copy(ending.at[batch], batches + batch, 0, {"section": entry, "group": 0})

    def set_up():
        loads[0].wait()
        loads[1].wait()

        @pl.when(first_section)
        def _():
            before_ref[...] = jnp.zeros_like(before_ref)
            blend[...] = jnp.zeros_like(blend)
            arrived[...] = jnp.zeros_like(arrived)

        @pl.when(jnp.logical_not(first_section))
        def _():
            all_bytes(before_ref, weight_recv).wait()
            share = units // tensor_count

            def product(pair, carry):
                rows = pl.ds(pl.multiple_of(pair * 2 * share, 2 * share), 2 * share)
                scaled = (before_ref[rows].astype(jnp.float32) * gain_ref[...]).astype(jnp.bfloat16)
                out = jnp.dot(scaled, win_ref[...], preferred_element_type=jnp.float32)
                blend_out[pl.ds(pair * 2, 2)] = out.astype(jnp.bfloat16).reshape(2, share, 2 * units)
                return carry

            lax.fori_loop(0, tensor_count // 2, product, 0)
            for offset in range(1, tensor_count):
                to_peer(
                    blend_out.at[(tensor + offset) % tensor_count], blend_in.at[offset - 1],
                    blend_send.at[0], blend_recv.at[0], offset,
                ).start()
            all_bytes(blend_in, blend_recv.at[0]).wait()
            total = blend_out[tensor].astype(jnp.float32)
            for offset in range(1, tensor_count):
                total += blend_in[offset - 1].astype(jnp.float32)
            blend[tensor] = total.astype(jnp.bfloat16)
            for offset in range(1, tensor_count):
                to_peer(
                    blend.at[tensor], blend.at[tensor], blend_send.at[1], blend_recv.at[1], offset
                ).start()

    def stage_a(batch):
        all_bytes(stream.at[batch], stream_recv.at[batch]).wait()
        scaled = (stream[batch].astype(jnp.float32) * gain_ref[...]).astype(jnp.bfloat16)
        mixed = jnp.dot(scaled, win_ref[...], preferred_element_type=jnp.float32)
        for half in range(2):
            rows = slice(half * HALF, (half + 1) * HALF)
            partial[batch, half] = jnp.concatenate(
                [mixed[rows, :units], mixed[rows, units:]], 0
            ).astype(jnp.bfloat16)
        for offset in range(1, tensor_count):
            to_peer(
                partial.at[batch, (tensor + offset) % 2], pieces.at[batch, offset - 1],
                piece_send.at[batch], piece_recv.at[batch], offset,
            ).start()

    def stage_c(batch):
        @pl.when(jnp.logical_not(first_section))
        def _():
            for half in range(2):
                all_bytes(arrived.at[batch, half], unit_recv.at[batch, half]).wait()

        hidden = jnp.concatenate([arrived[batch, 0], arrived[batch, 1]], 0)
        update = jnp.dot(hidden, before_ref[...], preferred_element_type=jnp.float32)
        fresh = (stream[batch].astype(jnp.float32) + update).astype(jnp.bfloat16)
        leaving[batch] = fresh

        @pl.when(jnp.logical_and(section > 0, jnp.logical_not(last_section)))
        def _():
            stream_copy(batch).start()

        values = fresh.astype(jnp.float32)
        squares = jnp.broadcast_to(jnp.sum(values * values, axis=1, keepdims=True), (ROWS, LANES))
        square_out[batch] = squares.reshape(2, HALF, LANES)
        for offset in range(1, tensor_count):
            to_peer(
                square_out.at[batch, (tensor + offset) % 2], square_in.at[batch, offset - 1],
                square_send.at[batch], square_recv.at[batch], offset,
            ).start()

    def stage_b(batch):
        @pl.when(jnp.logical_and(batch == 0, jnp.logical_not(first_section)))
        def _():
            all_bytes(blend.at[pl.ds(0, tensor_count - 1)], blend_recv.at[1]).wait()

        ahead = jnp.dot(
            arrived[batch, core],
            blend[...].reshape(units, 2 * units),
            preferred_element_type=jnp.float32,
        )
        all_bytes(pieces.at[batch], piece_recv.at[batch]).wait()
        total = partial[batch, core].astype(jnp.float32)
        for offset in range(1, tensor_count):
            total += pieces[batch, offset - 1].astype(jnp.float32)
        all_bytes(square_in.at[batch], square_recv.at[batch]).wait()
        squares = square_out[batch, core]
        for offset in range(1, tensor_count):
            squares += square_in[batch, offset - 1]
        scale = lax.rsqrt(squares[:, :1] / (width * tensor_count) + epsilon)
        gate = (total[:HALF] + ahead[:, :units]) * scale
        up = (total[HALF:] + ahead[:, units:]) * scale
        mine[batch] = (gate / (1.0 + jnp.exp(-gate)) * up).astype(jnp.bfloat16)

        @pl.when(jnp.logical_not(last_section))
        def _():
            unit_copy(batch, tensor).start()
            unit_copy(batch, twin).start()

        @pl.when(last_section)
        def _():
            twin_copy(batch).start()

    def stage_d(batch):
        twin_copy(batch).wait_recv()
        here, there = mine[batch], twin_rows[batch]
        hidden = jnp.concatenate(
            [jnp.where(core == 0, here, there), jnp.where(core == 0, there, here)], 0
        )
        update = jnp.dot(hidden, wout_ref[...], preferred_element_type=jnp.float32)
        ending[batch] = (leaving[batch].astype(jnp.float32) + update).astype(jnp.bfloat16)

        @pl.when(in_first)
        def _():
            final[batch] = ending[batch]
            for edge, (_, target) in enumerate(edges_a):
                final_copy(ending.at[batch], batch, edge, {"section": target}).start()

        @pl.when(in_second)
        def _():
            crossing_copy(batch).start()

    def relay():
        loads[2].wait()

        def step(index, carry):
            @pl.when(index < batches)
            def _():
                stage_a(index)

            @pl.when(index >= 1)
            def _():
                stage_b(index - 1)

            @pl.when(index < batches)
            def _():
                stage_c(index)

            @pl.when(jnp.logical_and(index >= 1, last_section))
            def _():
                stage_d(index - 1)

            return carry

        lax.fori_loop(0, batches + 1, step, 0)

    def pass_on(slot, edges, root):
        @pl.when(jnp.logical_not(root))
        def _():
            all_bytes(final.at[slot], final_recv.at[slot]).wait()

            @pl.when(in_first)
            def _():
                for edge, (sends, target) in enumerate(edges):
                    @pl.when(sends)
                    def _(edge=edge, target=target):
                        final_copy(final.at[slot], slot, edge, {"section": target}).start()

            @pl.when(jnp.logical_and(policy_passes, slot < batches))
            def _():
                final_copy(final.at[slot], slot, 0, {"section": across}).start()

    def logit_copy(chunk, offset):
        target = (tensor + offset) % tensor_count
        return pltpu.make_async_remote_copy(
            src_ref=logit_out.at[chunk, target],
            dst_ref=logit_in.at[chunk, offset - 1],
            send_sem=logit_send.at[chunk],
            recv_sem=logit_recv.at[chunk],
            device_id={"tensor": target},
            device_id_type=MESH,
        )

    def pol_copy(chunk):
        return pltpu.make_async_remote_copy(
            src_ref=pol_out.at[chunk],
            dst_ref=pol_in.at[chunk],
            send_sem=pol_send.at[chunk],
            recv_sem=pol_recv.at[chunk],
            device_id={"group": 1 - group},
            device_id_type=MESH,
        )

    per_chunk = CHUNK // ROWS

    def head_product(chunk):
        rows = jnp.concatenate(
            [
                final[pl.ds(chunk * per_chunk, per_chunk)].reshape(CHUNK, width),
                final[pl.ds(batches + chunk * per_chunk, per_chunk)].reshape(CHUNK, width),
            ],
            0,
        )
        logits = lax.dot_general(
            rows, head_ref[...], (((1,), (1,)), ((), ())), preferred_element_type=jnp.float32
        )
        logit_out[chunk] = logits.astype(jnp.bfloat16).reshape(
            tensor_count, 2 * CHUNK // tensor_count, vocab_block
        )
        for offset in range(1, tensor_count):
            logit_copy(chunk, offset).start()

    def head_total(chunk):
        all_bytes(logit_in.at[chunk], logit_recv.at[chunk]).wait()
        total = logit_out[chunk, tensor].astype(jnp.float32)
        for offset in range(1, tensor_count):
            total += logit_in[chunk, offset - 1].astype(jnp.float32)

        @pl.when(in_second)
        def _():
            pol_out[chunk] = total
            pol_copy(chunk).start()

        @pl.when(in_first)
        def _():
            pol_copy(chunk).wait_recv()
            pol = pol_in[chunk]
            rows = pl.ds(pl.multiple_of(chunk * BLOCK, BLOCK), BLOCK)
            ids = section * vocab_block + lax.broadcasted_iota(jnp.int32, pol.shape, 1)
            lane = lax.broadcasted_iota(jnp.int32, (BLOCK, LANES), 1)
            row = lax.broadcasted_iota(jnp.int32, (BLOCK, LANES), 0)
            first = (tensor % 2) * CHUNK + chunk * BLOCK
            samples = jnp.broadcast_to(sampled_ref[pl.ds(tensor // 2, 1), :], (BLOCK, LANES))
            wanted = jnp.sum(
                jnp.where(lane == first + row, samples.astype(jnp.float32), 0.0),
                axis=1, keepdims=True,
            ).astype(jnp.int32)
            picked = jnp.where(ids == wanted, pol, 0.0)
            peak_pol = jnp.max(pol, axis=1, keepdims=True)
            peak_ref = jnp.max(total, axis=1, keepdims=True)
            weights_pol = jnp.exp(pol - peak_pol)
            weights_ref = jnp.exp(total - peak_ref)
            stats = [
                peak_pol,
                peak_ref,
                jnp.sum(weights_pol, axis=1, keepdims=True),
                jnp.sum(weights_ref, axis=1, keepdims=True),
                jnp.sum(weights_pol * (pol - total), axis=1, keepdims=True),
                jnp.sum(picked, axis=1, keepdims=True),
            ]
            block = jnp.zeros((BLOCK, LANES), jnp.float32)
            for index, stat in enumerate(stats):
                block = jnp.where(lane == index, stat, block)
            stat_rows[rows, :] = block

    def head_work():
        loads[3].wait()
        loads[4].wait()
        stat_rows[...] = jnp.zeros_like(stat_rows)

        def step(index, carry):
            @pl.when(jnp.logical_and(index >= lag_a, index < batches + lag_a))
            def _():
                pass_on(index - lag_a, edges_a, jnp.logical_and(last_section, in_first))

            @pl.when(jnp.logical_and(index >= lag_b, index < batches + lag_b))
            def _():
                pass_on(batches + index - lag_b, edges_b, jnp.bool_(False))

            done = index - lag_most + 1
            chunk = done // per_chunk - 1
            full = jnp.logical_and(done > 0, done % per_chunk == 0)

            @pl.when(jnp.logical_and(full, chunk < chunks))
            def _():
                head_product(chunk)

            @pl.when(jnp.logical_and(full, jnp.logical_and(chunk >= 1, chunk <= chunks)))
            def _():
                head_total(chunk - 1)

            return carry

        lax.fori_loop(0, batches + lag_limit + per_chunk, step, 0)

    def stat_copy(to_section, to_group):
        return pltpu.make_async_remote_copy(
            src_ref=stat_out,
            dst_ref=stat_in.at[section],
            send_sem=stat_send,
            recv_sem=stat_recv,
            device_id={"section": to_section, "group": to_group},
            device_id_type=MESH,
        )

    @pl.when(policy_source)
    def _():
        send_policy()

    head_phase = jnp.where(policy_passes, 0, 2)
    set_up()

    def phase(index, carry):
        @pl.when(index == 1)
        def _():
            relay()

        @pl.when(index == head_phase)
        def _():
            head_work()

        return carry

    lax.fori_loop(0, 3, phase, 0)

    @pl.when(in_first)
    def _():
        block = jnp.transpose(stat_rows[...])[:8]
        stat_out[...] = block
        stat_in[section] = block
        for offset in range(section_count):
            to_section = (section + offset) % section_count
            if offset:
                stat_copy(to_section, 0).start()
            stat_copy(to_section, 1).start()

    def drain(batch, carry):
        all_bytes(pieces.at[batch], piece_send.at[batch]).wait()
        all_bytes(square_in.at[batch], square_send.at[batch]).wait()

        @pl.when(jnp.logical_not(last_section))
        def _():
            all_bytes(arrived.at[batch], unit_send.at[batch]).wait()

        @pl.when(last_section)
        def _():
            twin_copy(batch).wait_send()

        @pl.when(jnp.logical_and(section > 0, jnp.logical_not(last_section)))
        def _():
            stream_copy(batch).wait_send()

        @pl.when(in_first)
        def _():
            for first, edges in ((0, edges_a), (batches, edges_b)):
                for edge, (sends, target) in enumerate(edges):
                    @pl.when(sends)
                    def _(edge=edge, target=target, slot=first + batch):
                        final_copy(final.at[slot], slot, edge, {"section": target}).wait_send()

        @pl.when(policy_source)
        def _():
            for place in range(PER):
                policy_copy(batch * PER + place).wait_send()

        @pl.when(policy_passes)
        def _():
            final_copy(final.at[batch], batch, 0, {"section": across}).wait_send()

        @pl.when(crossing_out)
        def _():
            crossing_copy(batch).wait_send()

        return carry

    @pl.when(jnp.logical_not(last_section))
    def _():
        weight_copy.wait_send()

    @pl.when(jnp.logical_not(first_section))
    def _():
        for index in range(2):
            all_bytes(blend_in, blend_send.at[index]).wait()

    lax.fori_loop(0, batches, drain, 0)

    def drain_logits(chunk, carry):
        all_bytes(logit_in.at[chunk], logit_send.at[chunk]).wait()

        @pl.when(in_second)
        def _():
            pol_copy(chunk).wait_send()

        return carry

    lax.fori_loop(0, chunks, drain_logits, 0)

    @pl.when(in_first)
    def _():
        all_bytes(stat_in.at[pl.ds(0, section_count - 1)], stat_recv).wait()

    @pl.when(in_second)
    def _():
        all_bytes(stat_in.at[pl.ds(0, section_count)], stat_recv).wait()

    peaks_pol = [stat_in[index, 0:1] for index in range(section_count)]
    peaks_ref = [stat_in[index, 1:2] for index in range(section_count)]
    peak_pol, peak_ref = peaks_pol[0], peaks_ref[0]
    for index in range(1, section_count):
        peak_pol = jnp.maximum(peak_pol, peaks_pol[index])
        peak_ref = jnp.maximum(peak_ref, peaks_ref[index])
    total_pol = jnp.zeros_like(peak_pol)
    total_ref = jnp.zeros_like(peak_pol)
    cross = jnp.zeros_like(peak_pol)
    chosen = jnp.zeros_like(peak_pol)
    for index in range(section_count):
        shift_pol = jnp.exp(peaks_pol[index] - peak_pol)
        shift_ref = jnp.exp(peaks_ref[index] - peak_ref)
        total_pol += shift_pol * stat_in[index, 2:3]
        total_ref += shift_ref * stat_in[index, 3:4]
        cross += shift_pol * stat_in[index, 4:5]
        chosen += stat_in[index, 5:6]
    lse_pol = peak_pol + jnp.log(total_pol)
    lse_ref = peak_ref + jnp.log(total_ref)
    out_ref[0:1] = cross / total_pol - lse_pol + lse_ref
    out_ref[1:2] = chosen - lse_pol
    out_ref[2:] = jnp.zeros((6, LANES), jnp.float32)

    @pl.when(in_first)
    def _():
        all_bytes(stat_in.at[pl.ds(0, 2 * section_count - 1)], stat_send).wait()


def token_terms(rows, gain, weight_in, weight_out, policy_rows, head, sampled):
    tensor_count = lax.axis_size("tensor")
    section_count = lax.axis_size("section")
    blocks, _, width = rows.shape
    batches = blocks // PER
    units = weight_out.shape[0]
    vocab_block = head.shape[0]
    chunks = blocks * BLOCK // CHUNK
    share = units // tensor_count
    logit = (BLOCK, vocab_block)
    dma = pltpu.SemaphoreType.DMA
    vmem = pl.BlockSpec(memory_space=pltpu.VMEM)
    hbm = pl.BlockSpec(memory_space=pltpu.HBM)
    bf16, f32 = jnp.bfloat16, jnp.float32
    return pl.pallas_call(
        kernel,
        out_shape=jax.ShapeDtypeStruct((8, LANES), f32),
        in_specs=[hbm] * 7,
        out_specs=vmem,
        scratch_shapes=[
            pltpu.VMEM(gain.shape, f32),
            pltpu.VMEM(weight_in.shape, bf16),
            pltpu.VMEM(weight_out.shape, bf16),
            pltpu.VMEM(weight_out.shape, bf16),
            pltpu.VMEM(head.shape, bf16),
            pltpu.VMEM(sampled.shape, jnp.int32),
            pltpu.VMEM((tensor_count, share, 2 * units), bf16),
            pltpu.VMEM((tensor_count - 1, share, 2 * units), bf16),
            pltpu.VMEM((tensor_count, share, 2 * units), bf16),
            pltpu.VMEM((batches, ROWS, width), bf16),
            pltpu.VMEM((batches, 2, ROWS, units), bf16),
            pltpu.VMEM((batches, tensor_count - 1, ROWS, units), bf16),
            pltpu.VMEM((batches, 2, HALF, LANES), f32),
            pltpu.VMEM((batches, tensor_count - 1, HALF, LANES), f32),
            pltpu.VMEM((batches, HALF, units), bf16),
            pltpu.VMEM((batches, 2, HALF, units), bf16),
            pltpu.VMEM((batches, HALF, units), bf16),
            pltpu.VMEM((batches, ROWS, width), bf16),
            pltpu.VMEM((batches, ROWS, width), bf16),
            pltpu.VMEM((2 * batches, ROWS, width), bf16),
            pltpu.VMEM((chunks, tensor_count) + logit, bf16),
            pltpu.VMEM((chunks, tensor_count - 1) + logit, bf16),
            pltpu.VMEM((chunks,) + logit, f32),
            pltpu.VMEM((chunks,) + logit, f32),
            pltpu.VMEM((LANES, LANES), f32),
            pltpu.VMEM((8, LANES), f32),
            pltpu.VMEM((2 * section_count, 8, LANES), f32),
            dma((5,)),
            dma,
            dma,
            dma((2,)),
            dma((2,)),
            dma((batches,)),
            dma((batches,)),
            dma((batches,)),
            dma((batches,)),
            dma((batches,)),
            dma((batches, 2)),
            dma((batches,)),
            dma((batches,)),
            dma((batches,)),
            dma((batches,)),
            dma((2 * batches, 3)),
            dma((2 * batches,)),
            dma((blocks,)),
            dma((chunks,)),
            dma((chunks,)),
            dma((chunks,)),
            dma((chunks,)),
            dma,
            dma,
        ],
        compiler_params=pltpu.CompilerParams(
            collective_id=0, has_side_effects=True, vmem_limit_bytes=60 * 1024 * 1024
        ),
        name="token_terms",
    )(rows, gain, weight_in, weight_out, policy_rows, head, sampled)


def advantages(rewards, prompt_ids):
    same = (prompt_ids[:, None] == prompt_ids[None, :]).astype(jnp.float32)
    counts = jnp.sum(same, axis=1)
    means = jnp.sum(same * rewards[None, :], axis=1) / counts
    spread = rewards[None, :] - means[:, None]
    variance = jnp.sum(same * spread * spread, axis=1) / counts
    return (rewards - means) / jnp.maximum(jnp.sqrt(variance), 1.0)


def shards(
    ref_input, norm_gain, w_in, w_out, policy_hidden, heads, sampled, live_mask, rewards, prompt_ids
):
    tensor_here = lax.axis_index("tensor")
    group_count = lax.axis_size("group")
    group_here = lax.axis_index("group")
    tokens = sampled.shape[0]
    per_tensor = tokens // lax.axis_size("tensor")
    local_rows = per_tensor // group_count
    width = ref_input.shape[3]
    terms = token_terms(
        ref_input.reshape(-1, BLOCK, width),
        norm_gain,
        w_in[0],
        w_out[0],
        policy_hidden.reshape(-1, BLOCK, width),
        heads[0],
        sampled.reshape(-1, LANES),
    )
    terms = lax.dynamic_slice_in_dim(terms[:2], group_here * local_rows, local_rows, 1)
    token_kl, log_prob = terms[0], terms[1]
    row_start = (tensor_here * group_count + group_here) * local_rows
    token_adv = lax.dynamic_slice_in_dim(
        jnp.repeat(advantages(rewards, prompt_ids), RLEN), row_start, local_rows, 0
    )
    live = lax.dynamic_slice_in_dim(live_mask, row_start, local_rows, 0).astype(jnp.float32)
    token_loss = live * (penalty * token_kl - token_adv * log_prob) / RLEN
    return (token_kl, token_loss)


def solution(mesh):
    in_specs = (
        P("group", None, None, "tensor"),
        P("section", "tensor"),
        P("section", "tensor", None),
        P("section", None, "tensor"),
        P("group", "tensor"),
        P("group", "section", "tensor"),
        P(),
        P(),
        P(),
        P(),
    )
    out_specs = (P(("tensor", "group")), P(("tensor", "group")))
    return jax.shard_map(shards, mesh=mesh, in_specs=in_specs, out_specs=out_specs, check_vma=False)
```

```python
import jax
import jax.numpy as jnp
from jax import lax
from jax.experimental import pallas as pl
from jax.experimental.pallas import tpu as pltpu
from jax.sharding import PartitionSpec as P

RLEN = 64
SIDE = 4
BLOCK = 16
ROWS = 16
HALF = ROWS // 2
PER = ROWS // BLOCK
CHUNK = 64
PLAIN = 4
BEHIND = 2
FANOUT = 7
DIRECT = 12
LANES = 128

epsilon = 1e-05
penalty = 0.04
MESH = pl.DeviceIdType.MESH


def as_count(flag):
    return jnp.where(flag, 1, 0).astype(jnp.int32)


def block_at(place):
    return (place % SIDE) * SIDE + place // SIDE


def tree_edges(section, mirror):
    last = SIDE - 1
    row, column = section // SIDE, section % SIDE
    far = column if mirror else last - column
    step = 1 if mirror else -1
    root_row = 0 if mirror else last
    root = jnp.logical_and(far == 0, row == root_row)
    starts = jnp.logical_and(far == 0, row < last)
    chain = jnp.logical_and(far < last, row < last)
    below = jnp.logical_and(far > 0, row == last - 1)
    never = jnp.bool_(False)

    def to_row(r):
        return r * SIDE + column

    edges = [(root, root, to_row(r)) for r in ((2, 1, 3) if mirror else (2, 0, 1))]
    edges.append((below, below, to_row(last)))
    edges += [(never, starts, section + step * d) for d in (3, 2)]
    edges.append((chain, starts, section + step))
    delay = jnp.where(row == root_row, 0, 1) + far
    delay = delay + jnp.where(jnp.logical_and(far > 0, row == last), 1 if mirror else 2, 0)
    return edges, delay + (1 if mirror else 0)


def kernel(
    x_ref, gain_hbm, win_hbm, wout_hbm, policy_ref, head_hbm, sampled_hbm, out_ref,
    gain_ref, win_ref, wout_ref, before_ref, head_ref, sampled_ref,
    blend_out, blend_in, blend,
    stream, partial, pieces, square_out, square_in, mine, arrived, twin_rows, leaving, ending, final,
    logit_out, logit_in, pol_out, pol_in, stat_rows, stat_out, stat_in,
    load_sem, weight_send, weight_recv, blend_send, blend_recv,
    piece_send, piece_recv, square_send, square_recv, unit_send, unit_recv,
    twin_send, twin_recv, stream_send, stream_recv,
    final_send, final_recv, policy_send, logit_send, logit_recv, pol_send, pol_recv,
    stat_send, stat_recv,
):
    batches = stream.shape[0]
    width = stream.shape[2]
    units = wout_ref.shape[0]
    vocab_block = head_ref.shape[0]
    chunks = logit_out.shape[0]
    tensor_count = lax.axis_size("tensor")
    section_count = lax.axis_size("section")
    section = lax.axis_index("section")
    tensor = lax.axis_index("tensor")
    group = lax.axis_index("group")
    core = tensor % 2
    twin = tensor + 1 - 2 * core
    plain = section < PLAIN
    next_plain = section + 1 < PLAIN
    last_section = section == section_count - 1
    next_ahead = jnp.logical_not(jnp.logical_or(next_plain, last_section))
    closes = jnp.logical_or(next_plain, last_section)
    in_first = group == 0
    in_second = group == 1
    late_half = section >= section_count // 2
    edges_a, delay_a = tree_edges(section, False)
    edges_b, delay_b = tree_edges(section, True)
    lag = (delay_b - delay_a) * 3 // 2
    lag_a = jnp.where(in_first, jnp.maximum(-lag, 0), 0)
    lag_b = jnp.where(in_first, jnp.maximum(lag, 0), 0)
    lag_most = jnp.maximum(lag_a, lag_b)
    lag_limit = 9
    entry = 0
    crossing_out = jnp.logical_and(last_section, in_second)
    policy_source = jnp.logical_and(in_first, late_half)
    policy_passes = jnp.logical_and(in_second, late_half)
    across = (SIDE - 1 - section // SIDE) * SIDE + section % SIDE

    loads = [
        pltpu.make_async_copy(gain_hbm, gain_ref, load_sem.at[0]),
        pltpu.make_async_copy(win_hbm, win_ref, load_sem.at[1]),
        pltpu.make_async_copy(wout_hbm, wout_ref, load_sem.at[2]),
        pltpu.make_async_copy(head_hbm, head_ref, load_sem.at[3]),
        pltpu.make_async_copy(sampled_hbm, sampled_ref, load_sem.at[4]),
    ]

    def own_block(source, target, place, sem):
        return pltpu.make_async_copy(
            source.at[block_at(place)],
            target.at[place // PER, pl.ds((place % PER) * BLOCK, BLOCK)],
            sem.at[place // PER],
        )

    places = batches * PER

    @pl.when(section == 0)
    def _():
        def fetch(place, carry):
            own_block(x_ref, stream, place, stream_recv).start()
            return carry

        lax.fori_loop(0, places, fetch, 0)

    for load in loads:
        load.start()

    @pl.when(in_second)
    def _():
        def fetch(place, carry):
            pltpu.make_async_copy(
                policy_ref.at[block_at(place)],
                final.at[batches + place // PER, pl.ds((place % PER) * BLOCK, BLOCK)],
                final_recv.at[batches + place // PER],
            ).start()
            return carry

        lax.fori_loop(0, places, fetch, 0)

    barrier = pltpu.get_barrier_semaphore()

    def greet(where):
        pl.semaphore_signal(barrier, 1, device_id=where, device_id_type=MESH)

    for offset in range(1, tensor_count):
        greet({"tensor": (tensor + offset) % tensor_count})
    for offset in range(section_count):
        greet({"section": (section + offset) % section_count, "group": 1 - group})

    @pl.when(in_first)
    def _():
        for offset in range(1, section_count):
            greet({"section": (section + offset) % section_count})

    @pl.when(in_second)
    def _():
        greet({"section": across})

    @pl.when(jnp.logical_and(in_second, section > 0))
    def _():
        greet({"section": section - 1})

    @pl.when(jnp.logical_and(in_second, jnp.logical_not(last_section)))
    def _():
        greet({"section": section + 1})

    @pl.when(section > 0)
    def _():
        greet({"section": section - 1, "tensor": twin})

    @pl.when(jnp.logical_not(last_section))
    def _():
        greet({"section": section + 1, "tensor": twin})

    neighbours = as_count(section > 0) + as_count(jnp.logical_not(last_section))
    pl.semaphore_wait(
        barrier,
        tensor_count - 1 + section_count + neighbours + jnp.where(in_first, section_count - 1, neighbours + 1),
    )

    def all_bytes(ref, sem):
        return pltpu.make_async_copy(ref, ref, sem)

    def to_peer(source, target, send_sem, recv_sem, offset):
        return pltpu.make_async_remote_copy(
            src_ref=source,
            dst_ref=target,
            send_sem=send_sem,
            recv_sem=recv_sem,
            device_id={"tensor": (tensor + offset) % tensor_count},
            device_id_type=MESH,
        )

    weight_copy = pltpu.make_async_remote_copy(
        src_ref=wout_hbm,
        dst_ref=before_ref,
        send_sem=weight_send,
        recv_sem=weight_recv,
        device_id={"section": section + 1},
        device_id_type=MESH,
    )

    @pl.when(next_ahead)
    def _():
        weight_copy.start()

    def policy_copy(place):
        return pltpu.make_async_remote_copy(
            src_ref=policy_ref.at[block_at(place)],
            dst_ref=final.at[place // PER, pl.ds((place % PER) * BLOCK, BLOCK)],
            send_sem=policy_send.at[place],
            recv_sem=final_recv.at[place // PER],
            device_id={"group": 1 - group},
            device_id_type=MESH,
        )

    def send_policy():
        def one(place, carry):
            policy_copy(place).start()
            return carry

        lax.fori_loop(0, places, one, 0)

    def unit_copy(batch, where):
        return pltpu.make_async_remote_copy(
            src_ref=mine.at[batch],
            dst_ref=arrived.at[batch, core],
            send_sem=unit_send.at[batch],
            recv_sem=unit_recv.at[batch, core],
            device_id={"section": section + 1, "tensor": where},
            device_id_type=MESH,
        )

    def twin_copy(batch):
        return pltpu.make_async_remote_copy(
            src_ref=mine.at[batch],
            dst_ref=twin_rows.at[batch],
            send_sem=twin_send.at[batch],
            recv_sem=twin_recv.at[batch],
            device_id={"tensor": twin},
            device_id_type=MESH,
        )

    def stream_copy(batch, source):
        return pltpu.make_async_remote_copy(
            src_ref=source.at[batch],
            dst_ref=stream.at[batch],
            send_sem=stream_send.at[batch],
            recv_sem=stream_recv.at[batch],
            device_id={"section": section + 1},
            device_id_type=MESH,
        )

    def final_copy(source, slot, edge, where):
        return pltpu.make_async_remote_copy(
            src_ref=source,
            dst_ref=final.at[slot],
            send_sem=final_send.at[slot, edge],
            recv_sem=final_recv.at[slot],
            device_id=where,
            device_id_type=MESH,
        )

    def crossing_copy(batch):
        return final_copy(ending.at[batch], batches + batch, 0, {"section": entry, "group": 0})

    def sends_now(edge, batch):
        return jnp.logical_or(
            jnp.logical_and(batch < DIRECT, edge[0]), jnp.logical_and(batch >= DIRECT, edge[1])
        )

    def set_up():
        loads[0].wait()
        loads[1].wait()

        @pl.when(plain)
        def _():
            before_ref[...] = jnp.zeros_like(before_ref)
            blend[...] = jnp.zeros_like(blend)
            arrived[...] = jnp.zeros_like(arrived)

        @pl.when(jnp.logical_not(plain))
        def _():
            all_bytes(before_ref, weight_recv).wait()
            share = units // tensor_count

            def product(pair, carry):
                rows = pl.ds(pl.multiple_of(pair * 2 * share, 2 * share), 2 * share)
                scaled = (before_ref[rows].astype(jnp.float32) * gain_ref[...]).astype(jnp.bfloat16)
                out = jnp.dot(scaled, win_ref[...], preferred_element_type=jnp.float32)
                blend_out[pl.ds(pair * 2, 2)] = out.astype(jnp.bfloat16).reshape(2, share, 2 * units)
                return carry

            lax.fori_loop(0, tensor_count // 2, product, 0)
            for offset in range(1, tensor_count):
                to_peer(
                    blend_out.at[(tensor + offset) % tensor_count], blend_in.at[offset - 1],
                    blend_send.at[0], blend_recv.at[0], offset,
                ).start()
            all_bytes(blend_in, blend_recv.at[0]).wait()
            total = blend_out[tensor].astype(jnp.float32)
            for offset in range(1, tensor_count):
                total += blend_in[offset - 1].astype(jnp.float32)
            blend[tensor] = total.astype(jnp.bfloat16)
            for offset in range(1, tensor_count):
                to_peer(
                    blend.at[tensor], blend.at[tensor], blend_send.at[1], blend_recv.at[1], offset
                ).start()

    def stage_a(batch):
        all_bytes(stream.at[batch], stream_recv.at[batch]).wait()
        scaled = (stream[batch].astype(jnp.float32) * gain_ref[...]).astype(jnp.bfloat16)
        mixed = jnp.dot(scaled, win_ref[...], preferred_element_type=jnp.float32)
        for half in range(2):
            rows = slice(half * HALF, (half + 1) * HALF)
            partial[batch, half] = jnp.concatenate(
                [mixed[rows, :units], mixed[rows, units:]], 0
            ).astype(jnp.bfloat16)
        for offset in range(1, tensor_count):
            to_peer(
                partial.at[batch, (tensor + offset) % 2], pieces.at[batch, offset - 1],
                piece_send.at[batch], piece_recv.at[batch], offset,
            ).start()

    def stage_c(batch):
        @pl.when(jnp.logical_not(plain))
        def _():
            for half in range(2):
                all_bytes(arrived.at[batch, half], unit_recv.at[batch, half]).wait()

        hidden = jnp.concatenate([arrived[batch, 0], arrived[batch, 1]], 0).astype(jnp.bfloat16)
        update = jnp.dot(hidden, before_ref[...], preferred_element_type=jnp.float32)
        fresh = (stream[batch].astype(jnp.float32) + update).astype(jnp.bfloat16)
        leaving[batch] = fresh

        @pl.when(next_ahead)
        def _():
            stream_copy(batch, leaving).start()

        values = fresh.astype(jnp.float32)
        squares = jnp.broadcast_to(jnp.sum(values * values, axis=1, keepdims=True), (ROWS, LANES))
        square_out[batch] = squares.reshape(2, HALF, LANES)
        for offset in range(1, tensor_count):
            to_peer(
                square_out.at[batch, (tensor + offset) % 2], square_in.at[batch, offset - 1],
                square_send.at[batch], square_recv.at[batch], offset,
            ).start()

    def stage_b(batch):
        @pl.when(jnp.logical_and(batch == 0, jnp.logical_not(plain)))
        def _():
            all_bytes(blend.at[pl.ds(0, tensor_count - 1)], blend_recv.at[1]).wait()

        ahead = jnp.dot(
            arrived[batch, core].astype(jnp.bfloat16),
            blend[...].reshape(units, 2 * units),
            preferred_element_type=jnp.float32,
        )
        all_bytes(pieces.at[batch], piece_recv.at[batch]).wait()
        total = partial[batch, core].astype(jnp.float32)
        for offset in range(1, tensor_count):
            total += pieces[batch, offset - 1].astype(jnp.float32)
        all_bytes(square_in.at[batch], square_recv.at[batch]).wait()
        squares = square_out[batch, core]
        for offset in range(1, tensor_count):
            squares += square_in[batch, offset - 1]
        scale = lax.rsqrt(squares[:, :1] / (width * tensor_count) + epsilon)
        gate = (total[:HALF] + ahead[:, :units]) * scale
        up = (total[HALF:] + ahead[:, units:]) * scale
        mine[batch] = gate / (1.0 + jnp.exp(-gate)) * up

        @pl.when(next_ahead)
        def _():
            unit_copy(batch, tensor).start()
            unit_copy(batch, twin).start()

        @pl.when(closes)
        def _():
            twin_copy(batch).start()

    def stage_d(batch):
        twin_copy(batch).wait_recv()
        here, there = mine[batch], twin_rows[batch]
        hidden = jnp.concatenate(
            [jnp.where(core == 0, here, there), jnp.where(core == 0, there, here)], 0
        ).astype(jnp.bfloat16)
        update = jnp.dot(hidden, wout_ref[...], preferred_element_type=jnp.float32)
        ending[batch] = (leaving[batch].astype(jnp.float32) + update).astype(jnp.bfloat16)

        @pl.when(next_plain)
        def _():
            stream_copy(batch, ending).start()

        @pl.when(jnp.logical_and(last_section, in_first))
        def _():
            final[batch] = ending[batch]
            for edge, way in enumerate(edges_a):
                @pl.when(sends_now(way, batch))
                def _(edge=edge, target=way[2]):
                    final_copy(ending.at[batch], batch, edge, {"section": target}).start()

        @pl.when(crossing_out)
        def _():
            crossing_copy(batch).start()

    def relay():
        loads[2].wait()

        def step(index, carry):
            @pl.when(index < batches)
            def _():
                stage_a(index)

            @pl.when(index >= BEHIND)
            def _():
                stage_b(index - BEHIND)

            @pl.when(index < batches)
            def _():
                stage_c(index)

            @pl.when(jnp.logical_and(index >= BEHIND, closes))
            def _():
                stage_d(index - BEHIND)

            return carry

        lax.fori_loop(0, batches + BEHIND, step, 0)

    def pass_on(batch, slot, edges, root):
        @pl.when(jnp.logical_not(root))
        def _():
            all_bytes(final.at[slot], final_recv.at[slot]).wait()

            @pl.when(in_first)
            def _():
                for edge, way in enumerate(edges):
                    @pl.when(sends_now(way, batch))
                    def _(edge=edge, target=way[2]):
                        final_copy(final.at[slot], slot, edge, {"section": target}).start()

            @pl.when(jnp.logical_and(policy_passes, slot < batches))
            def _():
                final_copy(final.at[slot], slot, 0, {"section": across}).start()

    def logit_copy(chunk, offset):
        target = (tensor + offset) % tensor_count
        return pltpu.make_async_remote_copy(
            src_ref=logit_out.at[chunk, target],
            dst_ref=logit_in.at[chunk, offset - 1],
            send_sem=logit_send.at[chunk],
            recv_sem=logit_recv.at[chunk],
            device_id={"tensor": target},
            device_id_type=MESH,
        )

    def pol_copy(chunk):
        return pltpu.make_async_remote_copy(
            src_ref=pol_out.at[chunk],
            dst_ref=pol_in.at[chunk],
            send_sem=pol_send.at[chunk],
            recv_sem=pol_recv.at[chunk],
            device_id={"group": 1 - group},
            device_id_type=MESH,
        )

    per_chunk = CHUNK // ROWS

    def head_product(chunk):
        rows = jnp.concatenate(
            [
                final[pl.ds(chunk * per_chunk, per_chunk)].reshape(CHUNK, width),
                final[pl.ds(batches + chunk * per_chunk, per_chunk)].reshape(CHUNK, width),
            ],
            0,
        )
        logits = lax.dot_general(
            rows, head_ref[...], (((1,), (1,)), ((), ())), preferred_element_type=jnp.float32
        )
        logit_out[chunk] = logits.astype(jnp.bfloat16).reshape(
            tensor_count, 2 * CHUNK // tensor_count, vocab_block
        )
        for offset in range(1, tensor_count):
            logit_copy(chunk, offset).start()

    def head_total(chunk):
        all_bytes(logit_in.at[chunk], logit_recv.at[chunk]).wait()
        total = logit_out[chunk, tensor].astype(jnp.float32)
        for offset in range(1, tensor_count):
            total += logit_in[chunk, offset - 1].astype(jnp.float32)

        @pl.when(in_second)
        def _():
            pol_out[chunk] = total
            pol_copy(chunk).start()

        @pl.when(in_first)
        def _():
            pol_copy(chunk).wait_recv()
            pol = pol_in[chunk]
            rows = pl.ds(pl.multiple_of(chunk * BLOCK, BLOCK), BLOCK)
            ids = section * vocab_block + lax.broadcasted_iota(jnp.int32, pol.shape, 1)
            lane = lax.broadcasted_iota(jnp.int32, (BLOCK, LANES), 1)
            row = lax.broadcasted_iota(jnp.int32, (BLOCK, LANES), 0)
            first = (tensor % 2) * CHUNK + chunk * BLOCK
            samples = jnp.broadcast_to(sampled_ref[pl.ds(tensor // 2, 1), :], (BLOCK, LANES))
            wanted = jnp.sum(
                jnp.where(lane == first + row, samples.astype(jnp.float32), 0.0),
                axis=1, keepdims=True,
            ).astype(jnp.int32)
            picked = jnp.where(ids == wanted, pol, 0.0)
            peak_pol = jnp.max(pol, axis=1, keepdims=True)
            peak_ref = jnp.max(total, axis=1, keepdims=True)
            weights_pol = jnp.exp(pol - peak_pol)
            weights_ref = jnp.exp(total - peak_ref)
            stats = [
                peak_pol,
                peak_ref,
                jnp.sum(weights_pol, axis=1, keepdims=True),
                jnp.sum(weights_ref, axis=1, keepdims=True),
                jnp.sum(weights_pol * (pol - total), axis=1, keepdims=True),
                jnp.sum(picked, axis=1, keepdims=True),
            ]
            block = jnp.zeros((BLOCK, LANES), jnp.float32)
            for index, stat in enumerate(stats):
                block = jnp.where(lane == index, stat, block)
            stat_rows[rows, :] = block

    def head_work():
        loads[3].wait()
        loads[4].wait()
        stat_rows[...] = jnp.zeros_like(stat_rows)

        def step(index, carry):
            @pl.when(jnp.logical_and(index >= lag_a, index < batches + lag_a))
            def _():
                pass_on(index - lag_a, index - lag_a, edges_a, jnp.logical_and(last_section, in_first))

            @pl.when(jnp.logical_and(index >= lag_b, index < batches + lag_b))
            def _():
                pass_on(index - lag_b, batches + index - lag_b, edges_b, jnp.bool_(False))

            done = index - lag_most + 1
            chunk = done // per_chunk - 1
            full = jnp.logical_and(done > 0, done % per_chunk == 0)

            @pl.when(jnp.logical_and(full, chunk < chunks))
            def _():
                head_product(chunk)

            @pl.when(jnp.logical_and(full, jnp.logical_and(chunk >= 1, chunk <= chunks)))
            def _():
                head_total(chunk - 1)

            return carry

        lax.fori_loop(0, batches + lag_limit + per_chunk, step, 0)

    def stat_copy(to_section, to_group):
        return pltpu.make_async_remote_copy(
            src_ref=stat_out,
            dst_ref=stat_in.at[section],
            send_sem=stat_send,
            recv_sem=stat_recv,
            device_id={"section": to_section, "group": to_group},
            device_id_type=MESH,
        )

    @pl.when(policy_source)
    def _():
        send_policy()

    head_phase = jnp.where(policy_passes, 0, 2)
    set_up()

    def phase(index, carry):
        @pl.when(index == 1)
        def _():
            relay()

        @pl.when(index == head_phase)
        def _():
            head_work()

        return carry

    lax.fori_loop(0, 3, phase, 0)

    @pl.when(in_first)
    def _():
        block = jnp.transpose(stat_rows[...])[:8]
        stat_out[...] = block
        stat_in[section] = block
        for offset in range(section_count):
            to_section = (section + offset) % section_count
            if offset:
                stat_copy(to_section, 0).start()
            stat_copy(to_section, 1).start()

    def drain(batch, carry):
        all_bytes(pieces.at[batch], piece_send.at[batch]).wait()
        all_bytes(square_in.at[batch], square_send.at[batch]).wait()

        @pl.when(next_ahead)
        def _():
            all_bytes(arrived.at[batch], unit_send.at[batch]).wait()

        @pl.when(closes)
        def _():
            twin_copy(batch).wait_send()

        @pl.when(jnp.logical_not(last_section))
        def _():
            stream_copy(batch, leaving).wait_send()

        @pl.when(in_first)
        def _():
            for first, edges in ((0, edges_a), (batches, edges_b)):
                for edge, way in enumerate(edges):
                    @pl.when(sends_now(way, batch))
                    def _(edge=edge, target=way[2], slot=first + batch):
                        final_copy(final.at[slot], slot, edge, {"section": target}).wait_send()

        @pl.when(policy_source)
        def _():
            for place in range(PER):
                policy_copy(batch * PER + place).wait_send()

        @pl.when(policy_passes)
        def _():
            final_copy(final.at[batch], batch, 0, {"section": across}).wait_send()

        @pl.when(crossing_out)
        def _():
            crossing_copy(batch).wait_send()

        return carry

    @pl.when(next_ahead)
    def _():
        weight_copy.wait_send()

    @pl.when(jnp.logical_not(plain))
    def _():
        for index in range(2):
            all_bytes(blend_in, blend_send.at[index]).wait()

    lax.fori_loop(0, batches, drain, 0)

    def drain_logits(chunk, carry):
        all_bytes(logit_in.at[chunk], logit_send.at[chunk]).wait()

        @pl.when(in_second)
        def _():
            pol_copy(chunk).wait_send()

        return carry

    lax.fori_loop(0, chunks, drain_logits, 0)

    @pl.when(in_first)
    def _():
        all_bytes(stat_in.at[pl.ds(0, section_count - 1)], stat_recv).wait()

    @pl.when(in_second)
    def _():
        all_bytes(stat_in.at[pl.ds(0, section_count)], stat_recv).wait()

    peaks_pol = [stat_in[index, 0:1] for index in range(section_count)]
    peaks_ref = [stat_in[index, 1:2] for index in range(section_count)]
    peak_pol, peak_ref = peaks_pol[0], peaks_ref[0]
    for index in range(1, section_count):
        peak_pol = jnp.maximum(peak_pol, peaks_pol[index])
        peak_ref = jnp.maximum(peak_ref, peaks_ref[index])
    total_pol = jnp.zeros_like(peak_pol)
    total_ref = jnp.zeros_like(peak_pol)
    cross = jnp.zeros_like(peak_pol)
    chosen = jnp.zeros_like(peak_pol)
    for index in range(section_count):
        shift_pol = jnp.exp(peaks_pol[index] - peak_pol)
        shift_ref = jnp.exp(peaks_ref[index] - peak_ref)
        total_pol += shift_pol * stat_in[index, 2:3]
        total_ref += shift_ref * stat_in[index, 3:4]
        cross += shift_pol * stat_in[index, 4:5]
        chosen += stat_in[index, 5:6]
    lse_pol = peak_pol + jnp.log(total_pol)
    lse_ref = peak_ref + jnp.log(total_ref)
    out_ref[0:1] = cross / total_pol - lse_pol + lse_ref
    out_ref[1:2] = chosen - lse_pol
    out_ref[2:] = jnp.zeros((6, LANES), jnp.float32)

    @pl.when(in_first)
    def _():
        all_bytes(stat_in.at[pl.ds(0, 2 * section_count - 1)], stat_send).wait()


def token_terms(rows, gain, weight_in, weight_out, policy_rows, head, sampled):
    tensor_count = lax.axis_size("tensor")
    section_count = lax.axis_size("section")
    blocks, _, width = rows.shape
    batches = blocks // PER
    units = weight_out.shape[0]
    vocab_block = head.shape[0]
    chunks = blocks * BLOCK // CHUNK
    share = units // tensor_count
    logit = (BLOCK, vocab_block)
    dma = pltpu.SemaphoreType.DMA
    vmem = pl.BlockSpec(memory_space=pltpu.VMEM)
    hbm = pl.BlockSpec(memory_space=pltpu.HBM)
    bf16, f32 = jnp.bfloat16, jnp.float32
    return pl.pallas_call(
        kernel,
        out_shape=jax.ShapeDtypeStruct((8, LANES), f32),
        in_specs=[hbm] * 7,
        out_specs=vmem,
        scratch_shapes=[
            pltpu.VMEM(gain.shape, f32),
            pltpu.VMEM(weight_in.shape, bf16),
            pltpu.VMEM(weight_out.shape, bf16),
            pltpu.VMEM(weight_out.shape, bf16),
            pltpu.VMEM(head.shape, bf16),
            pltpu.VMEM(sampled.shape, jnp.int32),
            pltpu.VMEM((tensor_count, share, 2 * units), bf16),
            pltpu.VMEM((tensor_count - 1, share, 2 * units), bf16),
            pltpu.VMEM((tensor_count, share, 2 * units), bf16),
            pltpu.VMEM((batches, ROWS, width), bf16),
            pltpu.VMEM((batches, 2, ROWS, units), bf16),
            pltpu.VMEM((batches, tensor_count - 1, ROWS, units), bf16),
            pltpu.VMEM((batches, 2, HALF, LANES), f32),
            pltpu.VMEM((batches, tensor_count - 1, HALF, LANES), f32),
            pltpu.VMEM((batches, HALF, units), f32),
            pltpu.VMEM((batches, 2, HALF, units), f32),
            pltpu.VMEM((batches, HALF, units), f32),
            pltpu.VMEM((batches, ROWS, width), bf16),
            pltpu.VMEM((batches, ROWS, width), bf16),
            pltpu.VMEM((2 * batches, ROWS, width), bf16),
            pltpu.VMEM((chunks, tensor_count) + logit, bf16),
            pltpu.VMEM((chunks, tensor_count - 1) + logit, bf16),
            pltpu.VMEM((chunks,) + logit, f32),
            pltpu.VMEM((chunks,) + logit, f32),
            pltpu.VMEM((LANES, LANES), f32),
            pltpu.VMEM((8, LANES), f32),
            pltpu.VMEM((2 * section_count, 8, LANES), f32),
            dma((5,)),
            dma,
            dma,
            dma((2,)),
            dma((2,)),
            dma((batches,)),
            dma((batches,)),
            dma((batches,)),
            dma((batches,)),
            dma((batches,)),
            dma((batches, 2)),
            dma((batches,)),
            dma((batches,)),
            dma((batches,)),
            dma((batches,)),
            dma((2 * batches, FANOUT)),
            dma((2 * batches,)),
            dma((blocks,)),
            dma((chunks,)),
            dma((chunks,)),
            dma((chunks,)),
            dma((chunks,)),
            dma,
            dma,
        ],
        compiler_params=pltpu.CompilerParams(
            collective_id=0, has_side_effects=True, vmem_limit_bytes=60 * 1024 * 1024
        ),
        name="token_terms",
    )(rows, gain, weight_in, weight_out, policy_rows, head, sampled)


def advantages(rewards, prompt_ids):
    same = (prompt_ids[:, None] == prompt_ids[None, :]).astype(jnp.float32)
    counts = jnp.sum(same, axis=1)
    means = jnp.sum(same * rewards[None, :], axis=1) / counts
    spread = rewards[None, :] - means[:, None]
    variance = jnp.sum(same * spread * spread, axis=1) / counts
    return (rewards - means) / jnp.maximum(jnp.sqrt(variance), 1.0)


def shards(
    ref_input, norm_gain, w_in, w_out, policy_hidden, heads, sampled, live_mask, rewards, prompt_ids
):
    tensor_here = lax.axis_index("tensor")
    group_count = lax.axis_size("group")
    group_here = lax.axis_index("group")
    tokens = sampled.shape[0]
    per_tensor = tokens // lax.axis_size("tensor")
    local_rows = per_tensor // group_count
    width = ref_input.shape[3]
    terms = token_terms(
        ref_input.reshape(-1, BLOCK, width),
        norm_gain,
        w_in[0],
        w_out[0],
        policy_hidden.reshape(-1, BLOCK, width),
        heads[0],
        sampled.reshape(-1, LANES),
    )
    terms = lax.dynamic_slice_in_dim(terms[:2], group_here * local_rows, local_rows, 1)
    token_kl, log_prob = terms[0], terms[1]
    row_start = (tensor_here * group_count + group_here) * local_rows
    token_adv = lax.dynamic_slice_in_dim(
        jnp.repeat(advantages(rewards, prompt_ids), RLEN), row_start, local_rows, 0
    )
    live = lax.dynamic_slice_in_dim(live_mask, row_start, local_rows, 0).astype(jnp.float32)
    token_loss = live * (penalty * token_kl - token_adv * log_prob) / RLEN
    return (token_kl, token_loss)


def solution(mesh):
    in_specs = (
        P("group", None, None, "tensor"),
        P("section", "tensor"),
        P("section", "tensor", None),
        P("section", None, "tensor"),
        P("group", "tensor"),
        P("group", "section", "tensor"),
        P(),
        P(),
        P(),
        P(),
    )
    out_specs = (P(("tensor", "group")), P(("tensor", "group")))
    return jax.shard_map(shards, mesh=mesh, in_specs=in_specs, out_specs=out_specs, check_vma=False)
```

```python
import jax
import jax.numpy as jnp
from jax import lax
from jax.experimental import pallas as pl
from jax.experimental.pallas import tpu as pltpu
from jax.sharding import PartitionSpec as P

RLEN = 64
SIDE = 4
BLOCK = 16
ROWS = 16
HALF = ROWS // 2
PER = ROWS // BLOCK
CHUNK = 64
PLAIN = 6
BEHIND = 2
FANOUT = 7
DIRECT = 14
LANES = 128

epsilon = 1e-05
penalty = 0.04
MESH = pl.DeviceIdType.MESH


def as_count(flag):
    return jnp.where(flag, 1, 0).astype(jnp.int32)


def block_at(place):
    return (place % SIDE) * SIDE + place // SIDE


def tree_edges(section, mirror):
    last = SIDE - 1
    row, column = section // SIDE, section % SIDE
    far = column if mirror else last - column
    step = 1 if mirror else -1
    source = jnp.logical_and(far == 0, row == last)
    starts = jnp.logical_and(far == 0, row < last)
    chain = jnp.logical_and(far < last, row < last)
    never = jnp.bool_(False)

    def to_row(r):
        return (r % SIDE) * SIDE + column

    down = jnp.logical_and(far == 0, row < last - 1)
    edges = [(down, down, to_row(row + 1))]
    if mirror:
        ends = row == last - 1
        edges.append((ends, ends, to_row(last)))
        delay = row + 1 + far
    else:
        ends = jnp.logical_and(row == 0, far > 0)
        edges += [(ends, ends, to_row(last)), (source, source, to_row(0))]
        delay = jnp.where(row == last, jnp.where(far == 0, 0, 2 + far), row + 1 + far)
    edges += [(never, starts, section + step * d) for d in (3, 2)]
    edges.append((chain, starts, section + step))
    return edges, delay


def kernel(
    x_ref, gain_hbm, win_hbm, wout_hbm, policy_ref, head_hbm, sampled_hbm, out_ref,
    gain_ref, win_ref, wout_ref, before_ref, head_ref, sampled_ref,
    blend_out, blend_in, blend,
    stream, partial, pieces, square_out, square_in, mine, arrived, twin_rows, leaving, ending, final,
    logit_out, logit_in, pol_out, pol_in, stat_rows, stat_out, stat_in,
    load_sem, weight_send, weight_recv, blend_send, blend_recv,
    piece_send, piece_recv, square_send, square_recv, unit_send, unit_recv,
    twin_send, twin_recv, stream_send, stream_recv,
    final_send, final_recv, policy_send, logit_send, logit_recv, pol_send, pol_recv,
    stat_send, stat_recv,
):
    batches = stream.shape[0]
    width = stream.shape[2]
    units = wout_ref.shape[0]
    vocab_block = head_ref.shape[0]
    chunks = logit_out.shape[0]
    tensor_count = lax.axis_size("tensor")
    section_count = lax.axis_size("section")
    section = lax.axis_index("section")
    tensor = lax.axis_index("tensor")
    group = lax.axis_index("group")
    core = tensor % 2
    twin = tensor + 1 - 2 * core
    plain = section < PLAIN
    next_plain = section + 1 < PLAIN
    last_section = section == section_count - 1
    next_ahead = jnp.logical_not(jnp.logical_or(next_plain, last_section))
    closes = jnp.logical_or(next_plain, last_section)
    in_first = group == 0
    in_second = group == 1
    late_half = section >= section_count // 2
    edges_a, delay_a = tree_edges(section, False)
    edges_b, delay_b = tree_edges(section, True)
    lag = (delay_b - delay_a) * 3 // 2
    lag_a = jnp.where(in_first, jnp.maximum(-lag, 0), 0)
    lag_b = jnp.where(in_first, jnp.maximum(lag, 0), 0)
    lag_most = jnp.maximum(lag_a, lag_b)
    lag_limit = 10
    entry = 0
    crossing_out = jnp.logical_and(last_section, in_second)
    policy_source = jnp.logical_and(in_first, late_half)
    policy_passes = jnp.logical_and(in_second, late_half)
    across = (SIDE - 1 - section // SIDE) * SIDE + section % SIDE

    loads = [
        pltpu.make_async_copy(gain_hbm, gain_ref, load_sem.at[0]),
        pltpu.make_async_copy(win_hbm, win_ref, load_sem.at[1]),
        pltpu.make_async_copy(wout_hbm, wout_ref, load_sem.at[2]),
        pltpu.make_async_copy(head_hbm, head_ref, load_sem.at[3]),
        pltpu.make_async_copy(sampled_hbm, sampled_ref, load_sem.at[4]),
    ]

    def own_block(source, target, place, sem):
        return pltpu.make_async_copy(
            source.at[block_at(place)],
            target.at[place // PER, pl.ds((place % PER) * BLOCK, BLOCK)],
            sem.at[place // PER],
        )

    places = batches * PER

    @pl.when(section == 0)
    def _():
        def fetch(place, carry):
            own_block(x_ref, stream, place, stream_recv).start()
            return carry

        lax.fori_loop(0, places, fetch, 0)

    for index in (2, 0, 1, 3, 4):
        loads[index].start()

    @pl.when(in_second)
    def _():
        def fetch(place, carry):
            pltpu.make_async_copy(
                policy_ref.at[block_at(place)],
                final.at[batches + place // PER, pl.ds((place % PER) * BLOCK, BLOCK)],
                final_recv.at[batches + place // PER],
            ).start()
            return carry

        lax.fori_loop(0, places, fetch, 0)

    barrier = pltpu.get_barrier_semaphore()

    def greet(where):
        pl.semaphore_signal(barrier, 1, device_id=where, device_id_type=MESH)

    for offset in range(1, tensor_count):
        greet({"tensor": (tensor + offset) % tensor_count})
    for offset in range(section_count):
        greet({"section": (section + offset) % section_count, "group": 1 - group})

    @pl.when(in_first)
    def _():
        for offset in range(1, section_count):
            greet({"section": (section + offset) % section_count})

    @pl.when(in_second)
    def _():
        greet({"section": across})

    @pl.when(jnp.logical_and(in_second, section > 0))
    def _():
        greet({"section": section - 1})

    @pl.when(jnp.logical_and(in_second, jnp.logical_not(last_section)))
    def _():
        greet({"section": section + 1})

    @pl.when(section > 0)
    def _():
        greet({"section": section - 1, "tensor": twin})

    @pl.when(jnp.logical_not(last_section))
    def _():
        greet({"section": section + 1, "tensor": twin})

    neighbours = as_count(section > 0) + as_count(jnp.logical_not(last_section))
    pl.semaphore_wait(
        barrier,
        tensor_count - 1 + section_count + neighbours + jnp.where(in_first, section_count - 1, neighbours + 1),
    )

    def all_bytes(ref, sem):
        return pltpu.make_async_copy(ref, ref, sem)

    def to_peer(source, target, send_sem, recv_sem, offset):
        return pltpu.make_async_remote_copy(
            src_ref=source,
            dst_ref=target,
            send_sem=send_sem,
            recv_sem=recv_sem,
            device_id={"tensor": (tensor + offset) % tensor_count},
            device_id_type=MESH,
        )

    share = units // tensor_count

    def weight_copy(pair):
        rows = pl.ds(pl.multiple_of(pair * 2 * share, 2 * share), 2 * share)
        return pltpu.make_async_remote_copy(
            src_ref=wout_ref.at[rows],
            dst_ref=before_ref.at[rows],
            send_sem=weight_send.at[pair],
            recv_sem=weight_recv.at[pair],
            device_id={"section": section + 1},
            device_id_type=MESH,
        )

    loads[2].wait()

    @pl.when(next_ahead)
    def _():
        for pair in range(tensor_count // 2):
            weight_copy(pair).start()

    def policy_copy(place):
        return pltpu.make_async_remote_copy(
            src_ref=policy_ref.at[block_at(place)],
            dst_ref=final.at[place // PER, pl.ds((place % PER) * BLOCK, BLOCK)],
            send_sem=policy_send.at[place],
            recv_sem=final_recv.at[place // PER],
            device_id={"group": 1 - group},
            device_id_type=MESH,
        )

    def send_policy():
        def one(place, carry):
            policy_copy(place).start()
            return carry

        lax.fori_loop(0, places, one, 0)

    def unit_copy(batch, where):
        return pltpu.make_async_remote_copy(
            src_ref=mine.at[batch],
            dst_ref=arrived.at[batch, core],
            send_sem=unit_send.at[batch],
            recv_sem=unit_recv.at[batch, core],
            device_id={"section": section + 1, "tensor": where},
            device_id_type=MESH,
        )

    def twin_copy(batch):
        return pltpu.make_async_remote_copy(
            src_ref=mine.at[batch],
            dst_ref=twin_rows.at[batch],
            send_sem=twin_send.at[batch],
            recv_sem=twin_recv.at[batch],
            device_id={"tensor": twin},
            device_id_type=MESH,
        )

    def stream_copy(batch, source):
        return pltpu.make_async_remote_copy(
            src_ref=source.at[batch],
            dst_ref=stream.at[batch],
            send_sem=stream_send.at[batch],
            recv_sem=stream_recv.at[batch],
            device_id={"section": section + 1},
            device_id_type=MESH,
        )

    def final_copy(source, slot, edge, where):
        return pltpu.make_async_remote_copy(
            src_ref=source,
            dst_ref=final.at[slot],
            send_sem=final_send.at[slot, edge],
            recv_sem=final_recv.at[slot],
            device_id=where,
            device_id_type=MESH,
        )

    def crossing_copy(batch):
        return final_copy(ending.at[batch], batches + batch, 0, {"section": entry, "group": 0})

    def sends_now(edge, batch):
        return jnp.logical_or(
            jnp.logical_and(batch < DIRECT, edge[0]), jnp.logical_and(batch >= DIRECT, edge[1])
        )

    def set_up():
        loads[0].wait()
        loads[1].wait()

        @pl.when(plain)
        def _():
            before_ref[...] = jnp.zeros_like(before_ref)
            blend[...] = jnp.zeros_like(blend)
            arrived[...] = jnp.zeros_like(arrived)

        @pl.when(jnp.logical_not(plain))
        def _():
            def product(pair, carry):
                weight_copy(pair).wait_recv()
                rows = pl.ds(pl.multiple_of(pair * 2 * share, 2 * share), 2 * share)
                scaled = (before_ref[rows].astype(jnp.float32) * gain_ref[...]).astype(jnp.bfloat16)
                out = jnp.dot(scaled, win_ref[...], preferred_element_type=jnp.float32)
                blend_out[pl.ds(pair * 2, 2)] = out.astype(jnp.bfloat16).reshape(2, share, 2 * units)
                for side in range(2):
                    target = pair * 2 + side
                    offset = (target + tensor_count - tensor) % tensor_count

                    @pl.when(offset > 0)
                    def _(target=target, offset=offset):
                        to_peer(
                            blend_out.at[target], blend_in.at[offset - 1],
                            blend_send.at[0], blend_recv.at[0], offset,
                        ).start()

                return carry

            lax.fori_loop(0, tensor_count // 2, product, 0)
            all_bytes(blend_in, blend_recv.at[0]).wait()
            total = blend_out[tensor].astype(jnp.float32)
            for offset in range(1, tensor_count):
                total += blend_in[offset - 1].astype(jnp.float32)
            blend[tensor] = total.astype(jnp.bfloat16)
            for offset in range(1, tensor_count):
                to_peer(
                    blend.at[tensor], blend.at[tensor], blend_send.at[1], blend_recv.at[1], offset
                ).start()

    def stage_a(batch):
        all_bytes(stream.at[batch], stream_recv.at[batch]).wait()
        scaled = (stream[batch].astype(jnp.float32) * gain_ref[...]).astype(jnp.bfloat16)
        mixed = jnp.dot(scaled, win_ref[...], preferred_element_type=jnp.float32)
        for half in range(2):
            rows = slice(half * HALF, (half + 1) * HALF)
            partial[batch, half] = jnp.concatenate(
                [mixed[rows, :units], mixed[rows, units:]], 0
            ).astype(jnp.bfloat16)
        for offset in range(1, tensor_count):
            to_peer(
                partial.at[batch, (tensor + offset) % 2], pieces.at[batch, offset - 1],
                piece_send.at[batch], piece_recv.at[batch], offset,
            ).start()

    def stage_c(batch):
        @pl.when(jnp.logical_not(plain))
        def _():
            for half in range(2):
                all_bytes(arrived.at[batch, half], unit_recv.at[batch, half]).wait()

        hidden = jnp.concatenate([arrived[batch, 0], arrived[batch, 1]], 0).astype(jnp.bfloat16)
        update = jnp.dot(hidden, before_ref[...], preferred_element_type=jnp.float32)
        fresh = (stream[batch].astype(jnp.float32) + update).astype(jnp.bfloat16)
        leaving[batch] = fresh

        @pl.when(next_ahead)
        def _():
            stream_copy(batch, leaving).start()

        values = fresh.astype(jnp.float32)
        squares = jnp.broadcast_to(jnp.sum(values * values, axis=1, keepdims=True), (ROWS, LANES))
        square_out[batch] = squares.reshape(2, HALF, LANES)
        for offset in range(1, tensor_count):
            to_peer(
                square_out.at[batch, (tensor + offset) % 2], square_in.at[batch, offset - 1],
                square_send.at[batch], square_recv.at[batch], offset,
            ).start()

    def stage_b(batch):
        @pl.when(jnp.logical_and(batch == 0, jnp.logical_not(plain)))
        def _():
            all_bytes(blend.at[pl.ds(0, tensor_count - 1)], blend_recv.at[1]).wait()

        ahead = jnp.dot(
            arrived[batch, core].astype(jnp.bfloat16),
            blend[...].reshape(units, 2 * units),
            preferred_element_type=jnp.float32,
        )
        all_bytes(pieces.at[batch], piece_recv.at[batch]).wait()
        total = partial[batch, core].astype(jnp.float32)
        for offset in range(1, tensor_count):
            total += pieces[batch, offset - 1].astype(jnp.float32)
        all_bytes(square_in.at[batch], square_recv.at[batch]).wait()
        squares = square_out[batch, core]
        for offset in range(1, tensor_count):
            squares += square_in[batch, offset - 1]
        scale = lax.rsqrt(squares[:, :1] / (width * tensor_count) + epsilon)
        gate = (total[:HALF] + ahead[:, :units]) * scale
        up = (total[HALF:] + ahead[:, units:]) * scale
        mine[batch] = gate / (1.0 + jnp.exp(-gate)) * up

        @pl.when(next_ahead)
        def _():
            unit_copy(batch, tensor).start()
            unit_copy(batch, twin).start()

        @pl.when(closes)
        def _():
            twin_copy(batch).start()

    def stage_d(batch):
        twin_copy(batch).wait_recv()
        here, there = mine[batch], twin_rows[batch]
        hidden = jnp.concatenate(
            [jnp.where(core == 0, here, there), jnp.where(core == 0, there, here)], 0
        ).astype(jnp.bfloat16)
        update = jnp.dot(hidden, wout_ref[...], preferred_element_type=jnp.float32)
        ending[batch] = (leaving[batch].astype(jnp.float32) + update).astype(jnp.bfloat16)

        @pl.when(next_plain)
        def _():
            stream_copy(batch, ending).start()

        @pl.when(jnp.logical_and(last_section, in_first))
        def _():
            final[batch] = ending[batch]
            for edge, way in enumerate(edges_a):
                @pl.when(sends_now(way, batch))
                def _(edge=edge, target=way[2]):
                    final_copy(ending.at[batch], batch, edge, {"section": target}).start()

        @pl.when(crossing_out)
        def _():
            crossing_copy(batch).start()

    def relay():
        def step(index, carry):
            @pl.when(index < batches)
            def _():
                stage_a(index)

            @pl.when(index >= BEHIND)
            def _():
                stage_b(index - BEHIND)

            @pl.when(index < batches)
            def _():
                stage_c(index)

            @pl.when(jnp.logical_and(index >= BEHIND, closes))
            def _():
                stage_d(index - BEHIND)

            return carry

        lax.fori_loop(0, batches + BEHIND, step, 0)

    def pass_on(batch, slot, edges, root):
        @pl.when(jnp.logical_not(root))
        def _():
            all_bytes(final.at[slot], final_recv.at[slot]).wait()

            @pl.when(in_first)
            def _():
                for edge, way in enumerate(edges):
                    @pl.when(sends_now(way, batch))
                    def _(edge=edge, target=way[2]):
                        final_copy(final.at[slot], slot, edge, {"section": target}).start()

            @pl.when(jnp.logical_and(policy_passes, slot < batches))
            def _():
                final_copy(final.at[slot], slot, 0, {"section": across}).start()

    def logit_copy(chunk, offset):
        target = (tensor + offset) % tensor_count
        return pltpu.make_async_remote_copy(
            src_ref=logit_out.at[chunk, target],
            dst_ref=logit_in.at[chunk, offset - 1],
            send_sem=logit_send.at[chunk],
            recv_sem=logit_recv.at[chunk],
            device_id={"tensor": target},
            device_id_type=MESH,
        )

    def pol_copy(chunk):
        return pltpu.make_async_remote_copy(
            src_ref=pol_out.at[chunk],
            dst_ref=pol_in.at[chunk],
            send_sem=pol_send.at[chunk],
            recv_sem=pol_recv.at[chunk],
            device_id={"group": 1 - group},
            device_id_type=MESH,
        )

    per_chunk = CHUNK // ROWS

    def head_product(chunk):
        rows = jnp.concatenate(
            [
                final[pl.ds(chunk * per_chunk, per_chunk)].reshape(CHUNK, width),
                final[pl.ds(batches + chunk * per_chunk, per_chunk)].reshape(CHUNK, width),
            ],
            0,
        )
        logits = lax.dot_general(
            rows, head_ref[...], (((1,), (1,)), ((), ())), preferred_element_type=jnp.float32
        )
        logit_out[chunk] = logits.astype(jnp.bfloat16).reshape(
            tensor_count, 2 * CHUNK // tensor_count, vocab_block
        )
        for offset in range(1, tensor_count):
            logit_copy(chunk, offset).start()

    def head_total(chunk):
        all_bytes(logit_in.at[chunk], logit_recv.at[chunk]).wait()
        total = logit_out[chunk, tensor].astype(jnp.float32)
        for offset in range(1, tensor_count):
            total += logit_in[chunk, offset - 1].astype(jnp.float32)

        @pl.when(in_second)
        def _():
            pol_out[chunk] = total
            pol_copy(chunk).start()

        @pl.when(in_first)
        def _():
            pol_copy(chunk).wait_recv()
            pol = pol_in[chunk]
            rows = pl.ds(pl.multiple_of(chunk * BLOCK, BLOCK), BLOCK)
            ids = section * vocab_block + lax.broadcasted_iota(jnp.int32, pol.shape, 1)
            lane = lax.broadcasted_iota(jnp.int32, (BLOCK, LANES), 1)
            row = lax.broadcasted_iota(jnp.int32, (BLOCK, LANES), 0)
            first = (tensor % 2) * CHUNK + chunk * BLOCK
            samples = jnp.broadcast_to(sampled_ref[pl.ds(tensor // 2, 1), :], (BLOCK, LANES))
            wanted = jnp.sum(
                jnp.where(lane == first + row, samples.astype(jnp.float32), 0.0),
                axis=1, keepdims=True,
            ).astype(jnp.int32)
            picked = jnp.where(ids == wanted, pol, 0.0)
            peak_pol = jnp.max(pol, axis=1, keepdims=True)
            peak_ref = jnp.max(total, axis=1, keepdims=True)
            weights_pol = jnp.exp(pol - peak_pol)
            weights_ref = jnp.exp(total - peak_ref)
            stats = [
                peak_pol,
                peak_ref,
                jnp.sum(weights_pol, axis=1, keepdims=True),
                jnp.sum(weights_ref, axis=1, keepdims=True),
                jnp.sum(weights_pol * (pol - total), axis=1, keepdims=True),
                jnp.sum(picked, axis=1, keepdims=True),
            ]
            block = jnp.zeros((BLOCK, LANES), jnp.float32)
            for index, stat in enumerate(stats):
                block = jnp.where(lane == index, stat, block)
            stat_rows[rows, :] = block

    def head_work():
        loads[3].wait()
        loads[4].wait()
        stat_rows[...] = jnp.zeros_like(stat_rows)

        def step(index, carry):
            @pl.when(jnp.logical_and(index >= lag_a, index < batches + lag_a))
            def _():
                pass_on(index - lag_a, index - lag_a, edges_a, jnp.logical_and(last_section, in_first))

            @pl.when(jnp.logical_and(index >= lag_b, index < batches + lag_b))
            def _():
                pass_on(index - lag_b, batches + index - lag_b, edges_b, jnp.bool_(False))

            done = index - lag_most + 1
            chunk = done // per_chunk - 1
            full = jnp.logical_and(done > 0, done % per_chunk == 0)

            @pl.when(jnp.logical_and(full, chunk < chunks))
            def _():
                head_product(chunk)

            @pl.when(jnp.logical_and(full, jnp.logical_and(chunk >= 1, chunk <= chunks)))
            def _():
                head_total(chunk - 1)

            return carry

        lax.fori_loop(0, batches + lag_limit + per_chunk, step, 0)

    def stat_copy(to_section, to_group):
        return pltpu.make_async_remote_copy(
            src_ref=stat_out,
            dst_ref=stat_in.at[section],
            send_sem=stat_send,
            recv_sem=stat_recv,
            device_id={"section": to_section, "group": to_group},
            device_id_type=MESH,
        )

    @pl.when(policy_source)
    def _():
        send_policy()

    head_phase = jnp.where(policy_passes, 0, 2)
    set_up()

    def phase(index, carry):
        @pl.when(index == 1)
        def _():
            relay()

        @pl.when(index == head_phase)
        def _():
            head_work()

        return carry

    lax.fori_loop(0, 3, phase, 0)

    @pl.when(in_first)
    def _():
        block = jnp.transpose(stat_rows[...])[:8]
        stat_out[...] = block
        stat_in[section] = block
        for offset in range(section_count):
            to_section = (section + offset) % section_count
            if offset:
                stat_copy(to_section, 0).start()
            stat_copy(to_section, 1).start()

    def drain(batch, carry):
        all_bytes(pieces.at[batch], piece_send.at[batch]).wait()
        all_bytes(square_in.at[batch], square_send.at[batch]).wait()

        @pl.when(next_ahead)
        def _():
            all_bytes(arrived.at[batch], unit_send.at[batch]).wait()

        @pl.when(closes)
        def _():
            twin_copy(batch).wait_send()

        @pl.when(jnp.logical_not(last_section))
        def _():
            stream_copy(batch, leaving).wait_send()

        @pl.when(in_first)
        def _():
            for first, edges in ((0, edges_a), (batches, edges_b)):
                for edge, way in enumerate(edges):
                    @pl.when(sends_now(way, batch))
                    def _(edge=edge, target=way[2], slot=first + batch):
                        final_copy(final.at[slot], slot, edge, {"section": target}).wait_send()

        @pl.when(policy_source)
        def _():
            for place in range(PER):
                policy_copy(batch * PER + place).wait_send()

        @pl.when(policy_passes)
        def _():
            final_copy(final.at[batch], batch, 0, {"section": across}).wait_send()

        @pl.when(crossing_out)
        def _():
            crossing_copy(batch).wait_send()

        return carry

    @pl.when(next_ahead)
    def _():
        for pair in range(tensor_count // 2):
            weight_copy(pair).wait_send()

    @pl.when(jnp.logical_not(plain))
    def _():
        for index in range(2):
            all_bytes(blend_in, blend_send.at[index]).wait()

    lax.fori_loop(0, batches, drain, 0)

    def drain_logits(chunk, carry):
        all_bytes(logit_in.at[chunk], logit_send.at[chunk]).wait()

        @pl.when(in_second)
        def _():
            pol_copy(chunk).wait_send()

        return carry

    lax.fori_loop(0, chunks, drain_logits, 0)

    @pl.when(in_first)
    def _():
        all_bytes(stat_in.at[pl.ds(0, section_count - 1)], stat_recv).wait()

    @pl.when(in_second)
    def _():
        all_bytes(stat_in.at[pl.ds(0, section_count)], stat_recv).wait()

    peaks_pol = [stat_in[index, 0:1] for index in range(section_count)]
    peaks_ref = [stat_in[index, 1:2] for index in range(section_count)]
    peak_pol, peak_ref = peaks_pol[0], peaks_ref[0]
    for index in range(1, section_count):
        peak_pol = jnp.maximum(peak_pol, peaks_pol[index])
        peak_ref = jnp.maximum(peak_ref, peaks_ref[index])
    total_pol = jnp.zeros_like(peak_pol)
    total_ref = jnp.zeros_like(peak_pol)
    cross = jnp.zeros_like(peak_pol)
    chosen = jnp.zeros_like(peak_pol)
    for index in range(section_count):
        shift_pol = jnp.exp(peaks_pol[index] - peak_pol)
        shift_ref = jnp.exp(peaks_ref[index] - peak_ref)
        total_pol += shift_pol * stat_in[index, 2:3]
        total_ref += shift_ref * stat_in[index, 3:4]
        cross += shift_pol * stat_in[index, 4:5]
        chosen += stat_in[index, 5:6]
    lse_pol = peak_pol + jnp.log(total_pol)
    lse_ref = peak_ref + jnp.log(total_ref)
    out_ref[0:1] = cross / total_pol - lse_pol + lse_ref
    out_ref[1:2] = chosen - lse_pol
    out_ref[2:] = jnp.zeros((6, LANES), jnp.float32)

    @pl.when(in_first)
    def _():
        all_bytes(stat_in.at[pl.ds(0, 2 * section_count - 1)], stat_send).wait()


def token_terms(rows, gain, weight_in, weight_out, policy_rows, head, sampled):
    tensor_count = lax.axis_size("tensor")
    section_count = lax.axis_size("section")
    blocks, _, width = rows.shape
    batches = blocks // PER
    units = weight_out.shape[0]
    vocab_block = head.shape[0]
    chunks = blocks * BLOCK // CHUNK
    share = units // tensor_count
    logit = (BLOCK, vocab_block)
    dma = pltpu.SemaphoreType.DMA
    vmem = pl.BlockSpec(memory_space=pltpu.VMEM)
    hbm = pl.BlockSpec(memory_space=pltpu.HBM)
    bf16, f32 = jnp.bfloat16, jnp.float32
    return pl.pallas_call(
        kernel,
        out_shape=jax.ShapeDtypeStruct((8, LANES), f32),
        in_specs=[hbm] * 7,
        out_specs=vmem,
        scratch_shapes=[
            pltpu.VMEM(gain.shape, f32),
            pltpu.VMEM(weight_in.shape, bf16),
            pltpu.VMEM(weight_out.shape, bf16),
            pltpu.VMEM(weight_out.shape, bf16),
            pltpu.VMEM(head.shape, bf16),
            pltpu.VMEM(sampled.shape, jnp.int32),
            pltpu.VMEM((tensor_count, share, 2 * units), bf16),
            pltpu.VMEM((tensor_count - 1, share, 2 * units), bf16),
            pltpu.VMEM((tensor_count, share, 2 * units), bf16),
            pltpu.VMEM((batches, ROWS, width), bf16),
            pltpu.VMEM((batches, 2, ROWS, units), bf16),
            pltpu.VMEM((batches, tensor_count - 1, ROWS, units), bf16),
            pltpu.VMEM((batches, 2, HALF, LANES), f32),
            pltpu.VMEM((batches, tensor_count - 1, HALF, LANES), f32),
            pltpu.VMEM((batches, HALF, units), f32),
            pltpu.VMEM((batches, 2, HALF, units), f32),
            pltpu.VMEM((batches, HALF, units), f32),
            pltpu.VMEM((batches, ROWS, width), bf16),
            pltpu.VMEM((batches, ROWS, width), bf16),
            pltpu.VMEM((2 * batches, ROWS, width), bf16),
            pltpu.VMEM((chunks, tensor_count) + logit, bf16),
            pltpu.VMEM((chunks, tensor_count - 1) + logit, bf16),
            pltpu.VMEM((chunks,) + logit, f32),
            pltpu.VMEM((chunks,) + logit, f32),
            pltpu.VMEM((LANES, LANES), f32),
            pltpu.VMEM((8, LANES), f32),
            pltpu.VMEM((2 * section_count, 8, LANES), f32),
            dma((5,)),
            dma((tensor_count // 2,)),
            dma((tensor_count // 2,)),
            dma((2,)),
            dma((2,)),
            dma((batches,)),
            dma((batches,)),
            dma((batches,)),
            dma((batches,)),
            dma((batches,)),
            dma((batches, 2)),
            dma((batches,)),
            dma((batches,)),
            dma((batches,)),
            dma((batches,)),
            dma((2 * batches, FANOUT)),
            dma((2 * batches,)),
            dma((blocks,)),
            dma((chunks,)),
            dma((chunks,)),
            dma((chunks,)),
            dma((chunks,)),
            dma,
            dma,
        ],
        compiler_params=pltpu.CompilerParams(
            collective_id=0, has_side_effects=True, vmem_limit_bytes=60 * 1024 * 1024
        ),
        name="token_terms",
    )(rows, gain, weight_in, weight_out, policy_rows, head, sampled)


def advantages(rewards, prompt_ids):
    same = (prompt_ids[:, None] == prompt_ids[None, :]).astype(jnp.float32)
    counts = jnp.sum(same, axis=1)
    means = jnp.sum(same * rewards[None, :], axis=1) / counts
    spread = rewards[None, :] - means[:, None]
    variance = jnp.sum(same * spread * spread, axis=1) / counts
    return (rewards - means) / jnp.maximum(jnp.sqrt(variance), 1.0)


def shards(
    ref_input, norm_gain, w_in, w_out, policy_hidden, heads, sampled, live_mask, rewards, prompt_ids
):
    tensor_here = lax.axis_index("tensor")
    group_count = lax.axis_size("group")
    group_here = lax.axis_index("group")
    tokens = sampled.shape[0]
    per_tensor = tokens // lax.axis_size("tensor")
    local_rows = per_tensor // group_count
    width = ref_input.shape[3]
    terms = token_terms(
        ref_input.reshape(-1, BLOCK, width),
        norm_gain,
        w_in[0],
        w_out[0],
        policy_hidden.reshape(-1, BLOCK, width),
        heads[0],
        sampled.reshape(-1, LANES),
    )
    terms = lax.dynamic_slice_in_dim(terms[:2], group_here * local_rows, local_rows, 1)
    token_kl, log_prob = terms[0], terms[1]
    row_start = (tensor_here * group_count + group_here) * local_rows
    token_adv = lax.dynamic_slice_in_dim(
        jnp.repeat(advantages(rewards, prompt_ids), RLEN), row_start, local_rows, 0
    )
    live = lax.dynamic_slice_in_dim(live_mask, row_start, local_rows, 0).astype(jnp.float32)
    token_loss = live * (penalty * token_kl - token_adv * log_prob) / RLEN
    return (token_kl, token_loss)


def solution(mesh):
    in_specs = (
        P("group", None, None, "tensor"),
        P("section", "tensor"),
        P("section", "tensor", None),
        P("section", None, "tensor"),
        P("group", "tensor"),
        P("group", "section", "tensor"),
        P(),
        P(),
        P(),
        P(),
    )
    out_specs = (P(("tensor", "group")), P(("tensor", "group")))
    return jax.shard_map(shards, mesh=mesh, in_specs=in_specs, out_specs=out_specs, check_vma=False)
```
